32 devices in a mesh: groups: 2 (over y), dp: 4 (over z), tensor: 2 (over x), sub: 2 (over core).
Axes of the slice: x: 2, y: 2, z: 4, core: 2. Of those that a mesh axis runs over, the one named last changes fastest.
Arguments:
- token_input: bfloat16 [16, 16, 8192], P('dp', 'groups', ('tensor', 'sub')), parts along dimension 1, may hold values from -6 to 6
- gate_input: bfloat16 [16, 16, 8192], P('dp', 'groups', ('tensor', 'sub')), parts along dimension 1, may hold values from -6 to 6
- conv_taps: bfloat16 [16, 16, 3, 8192], P('dp', 'groups', None, ('tensor', 'sub')), parts along dimension 1, may hold values from -6 to 6
- scan_state: bfloat16 [16, 16, 16, 8192], P('dp', 'groups', None, ('tensor', 'sub')), parts along dimension 1, may hold values from -6 to 6
- conv_weight: bfloat16 [4, 8192], P(None, ('tensor', 'sub')), may hold values from -3 to 3
- conv_bias: float32 [8192], P(('tensor', 'sub')), may hold values from -3 to 3
- select_weight: bfloat16 [8192, 544], P(('tensor', 'sub')), may hold values from -0.0625 to 0.0625
- step_gain: float32 [512], replicated, may hold values from 0.1 to 1.9
- step_weight: bfloat16 [512, 8192], P(None, ('tensor', 'sub')), may hold values from -0.25 to 0.25
- step_bias: float32 [8192], P(('tensor', 'sub')), may hold values from -4.5 to -1
- decay_log: float32 [16, 8192], P(None, ('tensor', 'sub')), may hold values from 0 to 2.8
- skip_gain: float32 [8192], P(('tensor', 'sub')), may hold values from 0 to 2
- query: bfloat16 [16, 16, 8192], P('dp', ('groups', 'sub'), 'tensor'), parts along dimension 1, may hold values from -8 to 8
- fresh_key: bfloat16 [16, 16, 1024], P('dp', ('groups', 'sub'), 'tensor'), parts along dimension 1, may hold values from -6 to 6
- fresh_value: bfloat16 [16, 16, 1024], P('dp', ('groups', 'sub'), 'tensor'), parts along dimension 1, may hold values from -6 to 6
- key_cache: bfloat16 [16, 16, 256, 1024], P('dp', ('groups', 'sub'), None, 'tensor'), parts along dimension 1, may hold values from -6 to 6
- value_cache: bfloat16 [16, 16, 256, 1024], P('dp', ('groups', 'sub'), None, 'tensor'), parts along dimension 1, may hold values from -6 to 6
- cache_lengths: int32 [16, 16], P(None, 'groups'), parts along dimension 1, may hold values from 2 to 256, as said below
- parents: int32 [16, 16], P('groups'), parts along dimension 0, may hold values from 0 to 15
Outputs:
- next_state: bfloat16 [16, 16, 16, 8192], P('dp', 'groups', None, ('tensor', 'sub')), parts along dimension 1
- next_taps: bfloat16 [16, 16, 3, 8192], P('dp', 'groups', None, ('tensor', 'sub')), parts along dimension 1
- mamba_output: bfloat16 [16, 16, 8192], P('dp', 'groups', ('tensor', 'sub')), parts along dimension 1
- attention_output: bfloat16 [16, 16, 8192], P('dp', ('groups', 'sub'), 'tensor'), parts along dimension 1
The draws below stay inside these ranges and needn't reach their ends.
There are 2 independent parts, one for each index of `groups`. The reference program is written for one: setup_inputs(seed, part) draws one part's arguments, and reference() takes and returns one part's arrays. A program takes and returns all parts, laid end to end along the dimension named above; an argument that names none is the same for every part. Nothing has to cross between parts.
Inputs may be any that keep to these rules, and one draw needn't show every extreme that they name: cache_lengths[b, p] counts the live cache positions of beam b of prompt p, which are its first positions; in every draw some beam has all 256.
All inputs are finite; a program needn't handle non-finite values.
Results may differ from the reference program's by a relative error of at most 0.005.
Values may be sent and summed in bfloat16 or wider, within the bound.
No kernel may reach another device: no remote copies, remote signals or barrier semaphores. Data moves between devices by JAX's collectives and lax.ppermute only.
A program may use at most 128 MiB of HBM per device.

```python
import math
import jax
import jax.numpy as jnp
import numpy as np
from jax import lax

INNER = 8192
STATE = 16
DT_RANK = 512
CONV = 4
HEADS = 64
KV_HEADS = 8
HEAD_DIM = 128
BEAMS = 16
LEN = 256
PROMPTS = 8


def draw_query(key, part):
    key = jax.random.fold_in(key, 11)
    first_key = jax.random.fold_in(key, 0)
    shape = (BEAMS, PROMPTS, HEADS * HEAD_DIM)
    values = jnp.clip(1.5 * jax.random.normal(first_key, shape, jnp.float32), -6.0, 6.0)
    return values.astype(jnp.bfloat16)


def draw_key_cache(key, part):
    key = jax.random.fold_in(key, 12)
    first_key = jax.random.fold_in(key, 0)
    shape = (BEAMS, PROMPTS, LEN, KV_HEADS * HEAD_DIM)
    values = jnp.clip(1.5 * jax.random.normal(first_key, shape, jnp.float32), -6.0, 6.0)
    return values.astype(jnp.bfloat16)


def draw_cache_lengths(key, part):
    key = jax.random.fold_in(key, 13)
    first_key, second_key = jax.random.split(key)
    drawn = jax.random.randint(first_key, (BEAMS, PROMPTS), 2, LEN + 1, dtype=jnp.int32)
    spot = jax.random.randint(second_key, (), 0, BEAMS * PROMPTS, dtype=jnp.int32)
    flat = jnp.where(jnp.arange(BEAMS * PROMPTS, dtype=jnp.int32) == spot, LEN, drawn.reshape(BEAMS * PROMPTS))
    return flat.reshape(BEAMS, PROMPTS).astype(jnp.int32)


def plant(entries, own_key, low, top_value):
    extent = entries.shape
    place = [jax.random.randint(jax.random.fold_in(own_key, axis), (), 0, extent[axis]) for axis in range(len(extent))]
    entries = entries.at[tuple(place)].set(low)
    longest = extent.index(max(extent))
    place[longest] = (place[longest] + 1) % extent[longest]
    return entries.at[tuple(place)].set(top_value)


def block_scale(rng, shape, cuts, smallest, top_value):
    level, own = 1.0, jax.random.fold_in(rng, 6)
    for dim, shards_of in cuts:
        heights = jnp.exp(jax.random.uniform(jax.random.fold_in(own, dim), (shards_of,), jnp.float32, smallest / len(cuts), top_value / len(cuts)))
        level = level * jnp.repeat(heights, shape[dim] // shards_of).reshape([-1 if axis == dim else 1 for axis in range(len(shape))])
    return level


def rank_table(amount, lean):
    portions = [(1 << 20) // math.isqrt(standing ** lean) + 1 for standing in range(1, amount + 1)]
    spread = 1 + sum(portions) // (1 << 30)
    return np.cumsum(np.array([max(1, weight // spread) for weight in portions]))


def ranked_ids(stream_key, shape, number_of, lean):
    listing = rank_table(number_of, lean)
    pick = jax.random.randint(jax.random.fold_in(stream_key, 1), shape, 0, int(listing[number_of - 1]))
    standing = jnp.searchsorted(jnp.asarray(listing, jnp.int32), pick, side="right")
    return jax.random.permutation(jax.random.fold_in(stream_key, 2), number_of)[standing].astype(jnp.int32)


def normal_values(key, shape, spread, bound, pieces=(), kind=jnp.bfloat16):
    gain = block_scale(key, shape, pieces, -0.22, 0.18) if pieces else 1.0
    entries = jax.random.normal(key, shape, jnp.float32) * spread * gain
    return jnp.minimum(jnp.maximum(entries, -bound), bound).astype(kind)


def setup_inputs(seed: int = 0, part: int = 0) -> dict:
    arg_keys = jax.random.split(jax.random.key(seed), 20)
    part_keys = jax.random.split(jax.random.fold_in(arg_keys[19], part), 20)
    return {
        "token_input": normal_values(part_keys[0], (BEAMS, PROMPTS, INNER), 1.0, 6.0, ((0, 4), (2, 4))),
        "gate_input": normal_values(part_keys[1], (BEAMS, PROMPTS, INNER), 1.0, 6.0, ((0, 4), (2, 4))),
        "conv_taps": normal_values(part_keys[2], (BEAMS, PROMPTS, CONV - 1, INNER), 1.0, 6.0, ((0, 4), (3, 4))),
        "scan_state": normal_values(part_keys[3], (BEAMS, PROMPTS, STATE, INNER), 1.0, 6.0, ((0, 4), (3, 4))),
        "conv_weight": normal_values(arg_keys[4], (CONV, INNER), CONV ** -0.5, 3.0, ((1, 4),)),
        "conv_bias": normal_values(arg_keys[5], (INNER,), 0.5, 3.0, ((0, 4),), jnp.float32),
        "select_weight": normal_values(arg_keys[6], (INNER, DT_RANK + 2 * STATE), INNER ** -0.5, 0.0625, ((0, 4),)),
        "step_gain": jnp.clip(1.0 + 0.18 * jax.random.normal(arg_keys[7], (DT_RANK,), jnp.float32), 0.1, 1.9),
        "step_weight": normal_values(arg_keys[8], (DT_RANK, INNER), DT_RANK ** -0.5, 0.25, ((1, 4),)),
        "step_bias": jnp.clip(-4.5 + 3.5 * jax.random.uniform(arg_keys[9], (INNER,), jnp.float32) ** block_scale(arg_keys[9], (INNER,), ((0, 4),), -0.2, 0.2), -4.5, -1.0),
        "decay_log": jnp.clip(2.8 * jax.random.uniform(arg_keys[10], (STATE, INNER), jnp.float32) ** block_scale(arg_keys[10], (STATE, INNER), ((1, 4),), -0.2, 0.2), 0.0, 2.8),
        "skip_gain": jnp.clip(2.0 * jax.random.uniform(arg_keys[11], (INNER,), jnp.float32) ** block_scale(arg_keys[11], (INNER,), ((0, 4),), -0.2, 0.2), 0.0, 2.0),
        "query": draw_query(jax.random.fold_in(jax.random.fold_in(arg_keys[19], part), 71), part),
        "fresh_key": normal_values(part_keys[13], (BEAMS, PROMPTS, KV_HEADS * HEAD_DIM), 1.5, 6.0, ((0, 4), (1, 2), (2, 2))),
        "fresh_value": normal_values(part_keys[14], (BEAMS, PROMPTS, KV_HEADS * HEAD_DIM), 1.0, 6.0, ((0, 4), (1, 2), (2, 2))),
        "key_cache": draw_key_cache(jax.random.fold_in(jax.random.fold_in(arg_keys[19], part), 71), part),
        "value_cache": normal_values(part_keys[16], (BEAMS, PROMPTS, LEN, KV_HEADS * HEAD_DIM), 1.0, 6.0, ((0, 4), (1, 2), (3, 2))),
        "cache_lengths": draw_cache_lengths(jax.random.fold_in(jax.random.fold_in(arg_keys[19], part), 71), part),
        "parents": plant(ranked_ids(part_keys[18], (PROMPTS, BEAMS), BEAMS, 2), jax.random.fold_in(part_keys[18], 3), 0, BEAMS - 1).astype(jnp.int32),
    }


big_negative = -1e+30

def choose_rows(array, picks):
    index = picks.reshape(picks.shape + (1,) * (array.ndim - 2))
    return jnp.take_along_axis(array, index, axis=0)

def reference(token_input, gate_input, conv_taps, scan_state, conv_weight, conv_bias, select_weight, step_gain, step_weight, step_bias, decay_log, skip_gain, query, fresh_key, fresh_value, key_cache, value_cache, cache_lengths, parents):
    picks = parents.T.astype(jnp.int32)
    parent_taps = choose_rows(conv_taps, picks)
    parent_state = choose_rows(scan_state, picks)
    parent_length = jnp.take_along_axis(cache_lengths, picks, axis=0)
    window = jnp.concatenate([parent_taps, token_input[:, :, None, :]], axis=2)
    conv_output = jax.nn.silu(lax.optimization_barrier(jnp.sum(window.astype(jnp.float32) * conv_weight.astype(jnp.float32)[None, None], axis=2)) + conv_bias)
    conv_half = conv_output.astype(jnp.bfloat16)
    projected = jnp.dot(conv_half.reshape(BEAMS * PROMPTS, INNER), select_weight, preferred_element_type=jnp.float32)
    projected = projected.reshape(BEAMS, PROMPTS, DT_RANK + 2 * STATE)
    step_raw = projected[..., :DT_RANK]
    state_input = projected[..., DT_RANK:DT_RANK + STATE]
    state_readout = projected[..., DT_RANK + STATE:]
    step_norm = (step_raw * lax.rsqrt(lax.optimization_barrier(jnp.mean(step_raw * step_raw, axis=-1, keepdims=True)) + 1e-06) * step_gain).astype(jnp.bfloat16)
    step_size = jax.nn.softplus(jnp.dot(step_norm.reshape(BEAMS * PROMPTS, DT_RANK), step_weight, preferred_element_type=jnp.float32).reshape(BEAMS, PROMPTS, INNER) + step_bias)
    decay_factor = jnp.exp(-step_size[:, :, None, :] * jnp.exp(decay_log)[None, None])
    state_next = decay_factor * parent_state.astype(jnp.float32) + step_size[:, :, None, :] * state_input[..., None] * conv_output[:, :, None, :]
    readout = lax.optimization_barrier(jnp.sum(state_readout[..., None] * state_next, axis=2)) + skip_gain * conv_output
    mamba_output = (readout * jax.nn.silu(gate_input.astype(jnp.float32))).astype(jnp.bfloat16)
    group_size = HEADS // KV_HEADS
    score_scale = HEAD_DIM ** (-0.5)
    prompt_ids = jnp.arange(PROMPTS, dtype=jnp.int32)
    positions = jnp.arange(LEN, dtype=jnp.int32)

    def attend_child(child):
        rows_of = picks[child]
        parent_keys = key_cache[rows_of, prompt_ids].reshape(PROMPTS, LEN, KV_HEADS, HEAD_DIM).astype(jnp.float32)
        parent_values = value_cache[rows_of, prompt_ids].reshape(PROMPTS, LEN, KV_HEADS, HEAD_DIM).astype(jnp.float32)
        queries = query[child].reshape(PROMPTS, KV_HEADS, group_size, HEAD_DIM).astype(jnp.float32)
        new_keys = fresh_key[child].reshape(PROMPTS, KV_HEADS, HEAD_DIM).astype(jnp.float32)
        new_values = fresh_value[child].reshape(PROMPTS, KV_HEADS, HEAD_DIM).astype(jnp.float32)
        scores = jnp.einsum('pkgd,ptkd->pkgt', queries, parent_keys) * score_scale
        live_mask = positions[None, None, None, :] < parent_length[child][:, None, None, None]
        fresh_score = jnp.einsum('pkgd,pkd->pkg', queries, new_keys) * score_scale
        row_max = jnp.maximum(lax.optimization_barrier(jnp.max(jnp.where(live_mask, scores, big_negative), axis=-1)), fresh_score)
        weights = jnp.where(live_mask, jnp.exp(scores - row_max[..., None]), 0.0)
        fresh_weight = jnp.exp(fresh_score - row_max)
        row_total = lax.optimization_barrier(jnp.sum(weights, axis=-1)) + fresh_weight
        weights_half = (weights / row_total[..., None]).astype(jnp.bfloat16)
        fresh_half = (fresh_weight / row_total).astype(jnp.bfloat16)
        attended = jnp.einsum('pkgt,ptkd->pkgd', weights_half.astype(jnp.float32), parent_values)
        attended = attended + fresh_half.astype(jnp.float32)[..., None] * new_values[:, :, None, :]
        return attended.reshape(PROMPTS, HEADS * HEAD_DIM).astype(jnp.bfloat16)
    attention_output = lax.map(attend_child, jnp.arange(BEAMS, dtype=jnp.int32))
    return (state_next.astype(jnp.bfloat16), window[:, :, 1:, :], mamba_output, attention_output)
```

```python
import functools

import jax
import jax.numpy as jnp
import numpy as np
from jax import lax
from jax.experimental import pallas as pl
from jax.experimental.pallas import tpu as pltpu
from jax.sharding import PartitionSpec as P

HEADS = 64
KV_HEADS = 8
HEAD_DIM = 128
GROUP = HEADS // KV_HEADS

big_negative = -1e30

TIERS = ((16, 12, 12), (18, 13, 13), (20, 15, 15), (24, 18, 18), (32, 32, 32))
VMEM = 48 * 1024 * 1024
TINY = pl.CostEstimate(flops=1000, bytes_accessed=1000, transcendentals=0)


def pairs(mask):
    return [(i, i ^ mask) for i in range(4)]


def send(x, mask):
    return lax.ppermute(x, "dp", pairs(mask))


def plan_kernel(me_ref, parents_ref, plan):
    me = me_ref[0]
    row = lax.broadcasted_iota(jnp.int32, (128, 1), 0)
    owner = row // 32
    child_owner = lax.broadcasted_iota(jnp.int32, (128, 16), 1) // 4
    prompt = lax.broadcasted_iota(jnp.int32, (128, 8), 1)
    spread = jnp.where(lax.broadcasted_iota(jnp.int32, (128, 8), 0) % 8 == prompt, 1.0, 0.0)
    tiled = jnp.dot(
        spread, parents_ref[...].astype(jnp.float32), preferred_element_type=jnp.float32
    ).astype(jnp.int32)
    equal = tiled == row // 8
    child_lane = lax.broadcasted_iota(jnp.int32, (128, 16), 1)
    chosen = child_lane == me * 4 + row // 8
    target = jnp.sum(jnp.where(chosen, tiled, 0), axis=1, keepdims=True) * 8 + row % 8

    def wanted(mask):
        hit = equal & (child_owner == (owner ^ mask))
        return jnp.max(jnp.where(hit, 1.0, 0.0), axis=1, keepdims=True)

    passed = wanted(3)
    crossing = wanted(2) * (1.0 - passed)
    beside = wanted(1)
    lane = lax.broadcasted_iota(jnp.int32, (128, 128), 1)
    down = lax.broadcasted_iota(jnp.int32, (128, 128), 0)
    flags = jnp.where(
        lane == 0, passed, jnp.where(lane == 1, crossing, jnp.where(lane == 2, beside, 0.0))
    )
    same = lane // 32 == down // 32
    before = jnp.where(same & (lane < down), 1.0, 0.0)
    ahead = jnp.dot(before, flags, preferred_element_type=jnp.float32)
    totals = jnp.dot(jnp.where(same, 1.0, 0.0), flags, preferred_element_type=jnp.float32)
    x_slot = jnp.where(
        passed > 0.0,
        ahead[:, 0:1],
        jnp.where(crossing > 0.0, totals[:, 0:1] + ahead[:, 1:2], -1.0),
    ).astype(jnp.int32)
    o_slot = jnp.where(beside > 0.0, ahead[:, 2:3], -1.0).astype(jnp.int32)
    mine = owner == me
    local = row % 32

    def listing(slot_of):
        hit = (slot_of == lane) & mine
        return jnp.max(jnp.where(hit, local, -1), axis=0, keepdims=True)

    place = jnp.where(
        mine,
        local,
        jnp.where(
            owner == (me ^ 2),
            32 + x_slot,
            jnp.where(owner == (me ^ 1), 64 + o_slot, 96 + x_slot),
        ),
    )
    place_across = jnp.sum(jnp.where(lane == down, place, 0), axis=0, keepdims=True)
    code_down = jnp.sum(jnp.where(lane == target, place_across, 0), axis=1, keepdims=True)
    code = jnp.sum(jnp.where(lane == down, code_down, 0), axis=0, keepdims=True)
    x_most = jnp.max(totals[:, 0:1] + totals[:, 1:2], axis=0, keepdims=True)
    f_most = jnp.max(totals[:, 0:1], axis=0, keepdims=True)
    o_most = jnp.max(totals[:, 2:3], axis=0, keepdims=True)
    tier = jnp.zeros((1, 1), jnp.int32)
    for c, f, o in TIERS[:-1]:
        over = (x_most > float(c)) | (f_most > float(f)) | (o_most > float(o))
        tier += jnp.where(over, 1, 0)
    handed = jnp.full((1, 1), TIERS[-1][1], jnp.int32)
    for index in range(len(TIERS) - 1):
        handed = jnp.where(tier == index, TIERS[index][1], handed)
    child = row < 32
    late = child & ((code_down >= 96) | ((code_down >= 32 + handed) & (code_down < 64)))
    early = child & jnp.logical_not(late)
    groups = jnp.where(
        lane == 0, jnp.where(early, 1.0, 0.0), jnp.where(lane == 1, jnp.where(late, 1.0, 0.0), 0.0)
    )
    earlier = jnp.where(lane < down, 1.0, 0.0)
    position = jnp.dot(earlier, groups, preferred_element_type=jnp.float32).astype(jnp.int32)
    amount = jnp.sum(groups, axis=0, keepdims=True).astype(jnp.int32)

    def members(index, group):
        hit = (position[:, index : index + 1] == lane) & group
        return jnp.max(jnp.where(hit, row, -1), axis=0, keepdims=True)

    plan[0:1, :] = listing(x_slot)
    plan[1:2, :] = listing(o_slot)
    plan[2:3, :] = code
    plan[3:4, :] = jnp.broadcast_to(tier, (1, 128))
    plan[4:5, :] = members(0, early)
    plan[5:6, :] = members(1, late)
    plan[6:7, :] = amount
    plan[7:8, :] = jnp.zeros((1, 128), jnp.int32)


def make_plan(parents, me):
    return pl.pallas_call(
        plan_kernel,
        in_specs=[pl.BlockSpec(memory_space=pltpu.SMEM), pl.BlockSpec(memory_space=pltpu.VMEM)],
        out_specs=pl.BlockSpec(memory_space=pltpu.VMEM),
        out_shape=jax.ShapeDtypeStruct((8, 128), jnp.int32),
        name="plan",
    )(me.reshape(1), parents)


def attend_kernel(heads, q_ref, k_ref, v_ref, lo_ref, hi_ref, *outs):
    lo = jnp.concatenate([lo_ref[0]] * GROUP, axis=0)
    hi = jnp.concatenate([hi_ref[0]] * GROUP, axis=0)
    beams, _, length, _ = k_ref.shape
    keys = beams * length
    column = lax.broadcasted_iota(jnp.int32, (16 * GROUP, keys), 1)
    live = (column >= lo) & (column < hi)
    local = (hi > lo).astype(jnp.float32)
    scale = HEAD_DIM**-0.5
    width = GROUP * HEAD_DIM
    key_base = heads * width
    value_base = key_base + heads * HEAD_DIM
    for k in range(heads):
        q = jnp.concatenate(
            [
                q_ref[0, :, k * width + g * HEAD_DIM : k * width + (g + 1) * HEAD_DIM]
                for g in range(GROUP)
            ],
            axis=0,
        )
        head = slice(k * HEAD_DIM, (k + 1) * HEAD_DIM)
        keys_here = k_ref[:, 0, :, head].reshape(keys, HEAD_DIM)
        values_here = v_ref[:, 0, :, head].reshape(keys, HEAD_DIM)
        new_key = q_ref[0, :, key_base + k * HEAD_DIM : key_base + (k + 1) * HEAD_DIM]
        new_value = q_ref[0, :, value_base + k * HEAD_DIM : value_base + (k + 1) * HEAD_DIM]
        scores = (
            lax.dot_general(
                q, keys_here, (((1,), (1,)), ((), ())), preferred_element_type=jnp.float32
            )
            * scale
        )
        new_keys = jnp.concatenate([new_key.astype(jnp.float32)] * GROUP, axis=0)
        new_values = jnp.concatenate([new_value.astype(jnp.float32)] * GROUP, axis=0)
        fresh = jnp.sum(q.astype(jnp.float32) * new_keys, axis=1, keepdims=True) * scale
        scores = jnp.where(live, scores, big_negative)
        top = jnp.maximum(jnp.max(scores, axis=1, keepdims=True), fresh)
        weights = jnp.exp(scores - top)
        fresh_weight = jnp.exp(fresh - top)
        share = 1.0 / (jnp.sum(weights, axis=1, keepdims=True) + fresh_weight)
        half = (weights * share).astype(jnp.bfloat16)
        fresh_half = (fresh_weight * share).astype(jnp.bfloat16).astype(jnp.float32)
        mixed = jnp.dot(half, values_here, preferred_element_type=jnp.float32)
        mixed = jnp.where(local > 0.0, mixed + fresh_half * new_values, 0.0).astype(jnp.bfloat16)
        for block in range(4):
            out = outs[block % 2]
            for g in range(GROUP):
                out[block // 2, 0, :, k * width + g * HEAD_DIM : k * width + (g + 1) * HEAD_DIM] = mixed[
                    g * 16 + 4 * block : g * 16 + 4 * block + 4
                ]


def attend(queries, keys, values, lo, hi):
    prompts, children, width = queries.shape
    beams, _, length, depth = keys.shape
    heads = depth // HEAD_DIM
    wide = heads * GROUP * HEAD_DIM
    spec = pl.BlockSpec((beams, 1, length, depth), lambda p: (0, p, 0, 0))
    bound = pl.BlockSpec((1, children, 1), lambda p: (p, 0, 0))
    return pl.pallas_call(
        functools.partial(attend_kernel, heads),
        grid=(prompts,),
        in_specs=[pl.BlockSpec((1, children, width), lambda p: (p, 0, 0)), spec, spec, bound, bound],
        out_specs=[pl.BlockSpec((2, 1, 4, wide), lambda p: (0, p, 0, 0))] * 2,
        out_shape=[jax.ShapeDtypeStruct((2, prompts, 4, wide), jnp.bfloat16)] * 2,
        compiler_params=pltpu.CompilerParams(vmem_limit_bytes=VMEM),
        cost_estimate=TINY,
        name="attend",
    )(queries, keys, values, lo, hi)


def one_hot(column, width):
    lane = lax.broadcasted_iota(jnp.int32, (column.shape[0], width), 1)
    return (lane == column).astype(jnp.bfloat16)


def pick(column, table):
    return jnp.dot(one_hot(column, table.shape[0]), table, preferred_element_type=jnp.float32)


def pack_taps_kernel(*refs):
    half = len(refs) // 2
    taps = refs[half][...]
    for column, out in zip(refs[:half], refs[half + 1 :]):
        out[...] = pick(column[...], taps).astype(jnp.bfloat16)


def pack_taps(tier, plan, taps):
    c, f, o = tier
    width = taps.shape[1]
    listings = [plan[0, :c], plan[1, :o]] + ([plan[0, :f]] if c > f else [])
    columns = [
        jnp.concatenate([jnp.where(base >= 0, base + 32 * k, -1) for k in range(3)])[:, None]
        for base in listings
    ]
    vmem = pl.BlockSpec(memory_space=pltpu.VMEM)
    outs = pl.pallas_call(
        pack_taps_kernel,
        in_specs=[vmem] * (len(columns) + 1),
        out_specs=[vmem] * len(columns),
        out_shape=[jax.ShapeDtypeStruct((x.shape[0], width), jnp.bfloat16) for x in columns],
        compiler_params=pltpu.CompilerParams(vmem_limit_bytes=VMEM),
        cost_estimate=TINY,
        name="pack_taps",
    )(*columns, taps)
    return outs if c > f else (*outs, outs[0])


def pack_kernel(tier, plan, state, *rest):
    c, f, o = tier
    sems = rest[-1]
    xa, out = rest[0], rest[-2]

    def copies(which, first, count, target, base):
        def start(s, _):
            row = jnp.maximum(plan[which, first + s], 0)
            pltpu.make_async_copy(state.at[row], target.at[s], sems.at[base + s]).start()
            return 0

        lax.fori_loop(0, count, start, 0)

    copies(0, 0, f, xa, 0)
    copies(1, 0, o, out, c)
    if c > f:
        copies(0, f, c - f, rest[1], f)

    def finish(s, _):
        pltpu.make_async_copy(state.at[0], xa.at[0], sems.at[s]).wait()
        return 0

    lax.fori_loop(0, c + o, finish, 0)


def pack(tier, plan, state):
    c, f, o = tier
    rows = [f] + ([c - f] if c > f else []) + [o]
    vmem = pl.BlockSpec(memory_space=pltpu.VMEM)
    anywhere = pl.BlockSpec(memory_space=pl.ANY)
    outs = pl.pallas_call(
        functools.partial(pack_kernel, tier),
        in_specs=[pl.BlockSpec(memory_space=pltpu.SMEM), vmem],
        out_specs=[anywhere] * len(rows),
        out_shape=[jax.ShapeDtypeStruct((n,) + state.shape[1:], jnp.bfloat16) for n in rows],
        scratch_shapes=[pltpu.SemaphoreType.DMA((c + o,))],
        compiler_params=pltpu.CompilerParams(vmem_limit_bytes=VMEM),
        cost_estimate=TINY,
        name="pack",
    )(plan, state)
    if c == f:
        return outs[0], None, outs[1]
    return outs


def conv_kernel(code, token, weight, bias, select, taps, *rest):
    *tables, conv_out, next_taps, partial = rest
    count = token.shape[0]
    code = code[...]
    tap = lax.broadcasted_iota(jnp.int32, (3 * count, 1), 0) // count

    def part(base, table):
        size = table.shape[0] // 3
        slot = code - base
        inside = (slot >= 0) & (slot < size)
        return pick(jnp.where(inside, slot + tap * size, -1), table[...])

    window = part(0, taps)
    for index, table in enumerate(tables):
        window += part(32 * (index + 1), table)
    fresh = token[...]
    next_taps[0 : 2 * count, :] = window[count:].astype(jnp.bfloat16)
    next_taps[2 * count :, :] = fresh
    w = weight[...].astype(jnp.float32)
    total = window[:count] * w[0:1]
    total += window[count : 2 * count] * w[1:2]
    total += window[2 * count :] * w[2:3]
    total += fresh.astype(jnp.float32) * w[3:4]
    v = total + bias[...]
    conv = v / (1.0 + jnp.exp(-v))
    conv_out[...] = conv
    partial[...] = jnp.dot(
        conv.astype(jnp.bfloat16), select[...], preferred_element_type=jnp.float32
    )


def convolve(code, token, weight, bias, select, taps, tables):
    count, width = token.shape
    vmem = pl.BlockSpec(memory_space=pltpu.VMEM)
    return pl.pallas_call(
        conv_kernel,
        in_specs=[vmem] * (6 + len(tables)),
        out_specs=[vmem] * 3,
        out_shape=[
            jax.ShapeDtypeStruct((count, width), jnp.float32),
            jax.ShapeDtypeStruct((3 * count, width), jnp.bfloat16),
            jax.ShapeDtypeStruct((count, select.shape[1]), jnp.float32),
        ],
        compiler_params=pltpu.CompilerParams(vmem_limit_bytes=VMEM),
        cost_estimate=TINY,
        name="convolve",
    )(code, token, weight, bias, select, taps, *tables)


def step_kernel(projected, across, gain, weight, bias, step, b_wide, c_wide):
    rank = gain.shape[1]
    raw = projected[:, :rank]
    mean = jnp.mean(raw * raw, axis=1, keepdims=True)
    norm = (raw * lax.rsqrt(mean + 1e-06) * gain[...]).astype(jnp.bfloat16)
    v = jnp.dot(norm, weight[...], preferred_element_type=jnp.float32) + bias[...]
    step[...] = jnp.maximum(v, 0.0) + jnp.log1p(jnp.exp(-jnp.abs(v)))
    states = b_wide.shape[1]
    for r in range(b_wide.shape[0]):
        b_wide[r] = jnp.broadcast_to(across[:states, r : r + 1], b_wide.shape[1:])
        c_wide[r] = jnp.broadcast_to(across[states:, r : r + 1], c_wide.shape[1:])


def step_sizes(projected, gain, weight, bias):
    count, width = projected.shape[0], weight.shape[1]
    rank = gain.shape[1]
    across = projected[:, rank:].T
    states = across.shape[0] // 2
    vmem = pl.BlockSpec(memory_space=pltpu.VMEM)
    wide = jax.ShapeDtypeStruct((count, states, 128), jnp.float32)
    return pl.pallas_call(
        step_kernel,
        in_specs=[vmem] * 5,
        out_specs=[vmem] * 3,
        out_shape=[jax.ShapeDtypeStruct((count, width), jnp.float32), wide, wide],
        compiler_params=pltpu.CompilerParams(vmem_limit_bytes=VMEM),
        cost_estimate=TINY,
        name="step_sizes",
    )(projected, across, gain, weight, bias)


def advance(plan, which, starts, step, conv, rates, b_in, c_in, held, done, lines, next_state, sems):
    total = plan[6, which]
    in_sems, out_sems = sems

    def begin(n, _):
        r = plan[4 + which, n]
        where = plan[2, r]
        for condition, source, base in starts:

            @pl.when(condition(where))
            def _(source=source, base=base):
                pltpu.make_async_copy(source.at[where - base], held.at[n], in_sems.at[n]).start()

        return 0

    lax.fori_loop(0, total, begin, 0)
    def work(n, _):
        r = plan[4 + which, n]
        pltpu.make_async_copy(next_state.at[0], held.at[n], in_sems.at[n]).wait()
        b = b_in[r]
        c_out = c_in[r]
        sizes = step[pl.ds(r, 1), :]
        gains = sizes * conv[pl.ds(r, 1), :]
        readouts = []
        for first in range(0, step.shape[1], 128):
            part = slice(first, first + 128)
            state = held[n, :, part].astype(jnp.float32)
            new = jnp.exp(-sizes[:, part] * rates[:, part]) * state + gains[:, part] * b
            done[n, :, part] = new.astype(jnp.bfloat16)
            readouts.append(jnp.sum(c_out * new, axis=0, keepdims=True))
        lines[pl.ds(r, 1), :] = lines[pl.ds(r, 1), :] + jnp.concatenate(readouts, axis=1)
        pltpu.make_async_copy(done.at[n], next_state.at[r], out_sems.at[n]).start()
        return 0

    lax.fori_loop(0, total, work, 0)

    def finish(n, _):
        pltpu.make_async_copy(done.at[n], next_state.at[0], out_sems.at[n]).wait()
        return 0

    lax.fori_loop(0, total, finish, 0)


def early_kernel(
    tier, plan, step, conv, decay_log, skip, gate, b_in, c_in, local, xa, beside, next_state, lines, opened, held, done, rates, *sems
):
    f = tier[1]
    rates[...] = jnp.exp(decay_log[...])
    lines[...] = skip[...] * conv[...]
    gates = gate[...].astype(jnp.float32)
    opened[...] = gates / (1.0 + jnp.exp(-gates))
    starts = (
        (lambda w: w < 32, local, 0),
        (lambda w: (w >= 32) & (w < 32 + f), xa, 32),
        (lambda w: (w >= 64) & (w < 96), beside, 64),
    )
    advance(plan, 0, starts, step, conv, rates, b_in, c_in, held, done, lines, next_state, sems)


def late_kernel(
    tier, has_xb, plan, step, conv, decay_log, b_in, c_in, lines_in, opened, *rest
):
    f = tier[1]
    sources, rest = rest[: 2 if has_xb else 1], rest[2 if has_xb else 1 :]
    _, next_state, output, held, done, rates, lines, *sems = rest
    rates[...] = jnp.exp(decay_log[...])
    lines[...] = lines_in[...]
    starts = [(lambda w: w >= 96, sources[-1], 96)]
    if has_xb:
        starts.append((lambda w: w < 96, sources[0], 32 + f))
    advance(plan, 1, starts, step, conv, rates, b_in, c_in, held, done, lines, next_state, sems)
    output[...] = (lines[...] * opened[...]).astype(jnp.bfloat16)


def scan_scratch(count, states, width):
    return [
        pltpu.VMEM((count, states, width), jnp.bfloat16),
        pltpu.VMEM((count, states, width), jnp.bfloat16),
        pltpu.VMEM((states, width), jnp.float32),
    ], [pltpu.SemaphoreType.DMA((count,)), pltpu.SemaphoreType.DMA((count,))]


def early(tier, plan, step, conv, decay_log, skip, gate, b_in, c_in, local, xa, beside):
    count, width = step.shape
    states = decay_log.shape[0]
    vmem = pl.BlockSpec(memory_space=pltpu.VMEM)
    anywhere = pl.BlockSpec(memory_space=pl.ANY)
    arrays, sems = scan_scratch(count, states, width)
    return pl.pallas_call(
        functools.partial(early_kernel, tier),
        in_specs=[pl.BlockSpec(memory_space=pltpu.SMEM)] + [vmem] * 7 + [anywhere] * 3,
        out_specs=[anywhere, vmem, vmem],
        out_shape=[
            jax.ShapeDtypeStruct((count, states, width), jnp.bfloat16),
            jax.ShapeDtypeStruct((count, width), jnp.float32),
            jax.ShapeDtypeStruct((count, width), jnp.float32),
        ],
        scratch_shapes=arrays + sems,
        compiler_params=pltpu.CompilerParams(vmem_limit_bytes=VMEM),
        cost_estimate=TINY,
        name="early",
    )(plan, step, conv, decay_log, skip, gate, b_in, c_in, local, xa, beside)


def late(tier, plan, step, conv, decay_log, b_in, c_in, lines, opened, buffers, next_state):
    count, width = step.shape
    states = decay_log.shape[0]
    vmem = pl.BlockSpec(memory_space=pltpu.VMEM)
    anywhere = pl.BlockSpec(memory_space=pl.ANY)
    arrays, sems = scan_scratch(count, states, width)
    return pl.pallas_call(
        functools.partial(late_kernel, tier, len(buffers) == 2),
        in_specs=[pl.BlockSpec(memory_space=pltpu.SMEM)]
        + [vmem] * 7
        + [anywhere] * (len(buffers) + 1),
        out_specs=[anywhere, vmem],
        out_shape=[
            jax.ShapeDtypeStruct((count, states, width), jnp.bfloat16),
            jax.ShapeDtypeStruct((count, width), jnp.bfloat16),
        ],
        scratch_shapes=arrays + [pltpu.VMEM((count, width), jnp.float32)] + sems,
        input_output_aliases={8 + len(buffers): 0},
        compiler_params=pltpu.CompilerParams(vmem_limit_bytes=VMEM),
        cost_estimate=TINY,
        name="late",
    )(plan, step, conv, decay_log, b_in, c_in, lines, opened, *buffers, next_state)


def swap(x, axis):
    size = lax.axis_size(axis)
    return x + lax.ppermute(x, axis, [(i, i ^ 1) for i in range(size)])


def quick_body(
    token_input,
    gate_input,
    conv_taps,
    scan_state,
    conv_weight,
    conv_bias,
    select_weight,
    step_gain,
    step_weight,
    step_bias,
    decay_log,
    skip_gain,
    query,
    fresh_key,
    fresh_value,
    key_cache,
    value_cache,
    cache_lengths,
    parents,
):
    me = lax.axis_index("dp")
    beams, prompts, width = token_input.shape
    states, rank = decay_log.shape[0], step_gain.shape[0]
    count = beams * prompts
    cache_prompts, length = key_cache.shape[1], key_cache.shape[2]
    first = lax.axis_index("sub") * cache_prompts

    fresh = jnp.concatenate([fresh_key, fresh_value], axis=2)
    asked = [query, send(query, 1), send(query, 2)]
    fresh = [fresh, send(fresh, 1), send(fresh, 2)]

    plan = make_plan(parents, me)
    here = lax.dynamic_slice_in_dim(parents, first, cache_prompts, 0)
    lengths = lax.dynamic_slice_in_dim(cache_lengths, first, cache_prompts, 1)
    related = jnp.concatenate(
        [lax.dynamic_slice_in_dim(here, (me ^ mask) * beams, beams, 1) for mask in range(4)], axis=1
    )
    live = jnp.sum(
        jnp.where(related[:, :, None] == np.arange(16)[None, None, :], lengths.T[:, None, :], 0), axis=2
    )
    local = related // beams == me
    lo = jnp.where(local, (related % beams) * length, 0)
    hi = jnp.where(local, lo + live, 0)
    lo, hi = lo[:, :, None], hi[:, :, None]
    taps = conv_taps.transpose(2, 0, 1, 3).reshape(3 * count, width)
    state = scan_state.reshape(count, states, width)
    code_column = jnp.tile(plan[2, :count], 3)[:, None]

    def run(limits):
        c, f, o = limits

        def branch(plan, code_column, taps, state, asked, fresh, lo, hi):
            asked = [*asked, send(asked[2], 1)]
            fresh = [*fresh, send(fresh[2], 1)]
            tx, to, tf = pack_taps(limits, plan, taps)
            tables = [send(tx, 2), send(to, 1), send(tf, 3)]
            xa, xb, near = pack(limits, plan, state)
            xa, near, *tables = lax.optimization_barrier((xa, near, *tables))
            xa, near = send(xa, 2), send(near, 1)
            conv, next_taps, partial = convolve(
                code_column,
                token_input.reshape(count, width),
                conv_weight,
                conv_bias[None],
                select_weight,
                taps,
                tables,
            )
            partial = swap(partial, "sub")
            asked = jnp.concatenate(asked, axis=0)
            fresh = jnp.concatenate(fresh, axis=0)
            queries = jnp.concatenate([asked, fresh], axis=2).transpose(1, 0, 2)
            queries, partial = lax.optimization_barrier((queries, partial))
            projected = swap(partial, "tensor")
            outs = attend(queries, key_cache, value_cache, lo, hi)
            step, b_in, c_in = step_sizes(projected, step_gain[None], step_weight, step_bias[None])
            second = [*outs] if xb is None else [*outs, xb]
            xa, near, step, *second = lax.optimization_barrier((xa, near, step, *second))
            passed = send(xa, 1)
            buffers = [passed] if xb is None else [send(second[2], 2), passed]
            back = second[0] + send(second[1], 1)
            attention = (back[0] + send(back[1], 2)).transpose(1, 0, 2)
            next_state, lines, opened = early(
                limits,
                plan,
                step,
                conv,
                decay_log,
                skip_gain[None],
                gate_input.reshape(count, width),
                b_in,
                c_in,
                state,
                xa,
                near,
            )
            next_state, output = late(
                limits, plan, step, conv, decay_log, b_in, c_in, lines, opened, buffers, next_state
            )
            next_taps = next_taps.reshape(3, beams, prompts, width).transpose(1, 2, 0, 3)
            return next_state, next_taps, output, attention

        return branch

    next_state, next_taps, output, attention = lax.switch(
        plan[3, 0],
        [run(limits) for limits in TIERS],
        plan,
        code_column,
        taps,
        state,
        asked,
        fresh,
        lo,
        hi,
    )
    return (
        next_state.reshape(beams, prompts, states, width),
        next_taps,
        output.reshape(beams, prompts, width),
        attention,
    )


def choose_rows(array, picks):
    index = picks.reshape(picks.shape + (1,) * (array.ndim - 2))
    return jnp.take_along_axis(array, index, axis=0)


def parent_rows(parents, first, count):
    return lax.dynamic_slice_in_dim(parents, first, count, 0).T


def general_body(
    token_input,
    gate_input,
    conv_taps,
    scan_state,
    conv_weight,
    conv_bias,
    select_weight,
    step_gain,
    step_weight,
    step_bias,
    decay_log,
    skip_gain,
    query,
    fresh_key,
    fresh_value,
    key_cache,
    value_cache,
    cache_lengths,
    parents,
):
    group_width = lax.axis_size("dp")
    my_index = lax.axis_index("dp")
    sub_index = lax.axis_index("sub")
    beam_slots = token_input.shape[0]
    prompt_count = token_input.shape[1]
    prompt_share = prompt_count // group_width
    cache_prompts = key_cache.shape[1]
    cache_share = cache_prompts // group_width
    cache_base = sub_index * cache_prompts
    cache_length = key_cache.shape[2]
    group_size = HEADS // KV_HEADS
    score_scale = HEAD_DIM ** (-0.5)
    heads_local = query.shape[2] // HEAD_DIM
    kv_local = fresh_key.shape[2] // HEAD_DIM
    state_picks = parent_rows(parents, my_index * prompt_share, prompt_share)
    cache_picks = parent_rows(parents, cache_base + my_index * cache_share, cache_share)
    local_lengths = lax.dynamic_slice_in_dim(cache_lengths, cache_base, cache_prompts, 1)
    prompt_parents = parent_rows(parents, cache_base, cache_prompts)
    positions = jnp.arange(cache_length, dtype=jnp.int32)
    arrived = (
        lax.all_to_all(conv_taps, "dp", split_axis=1, concat_axis=0, tiled=True),
        lax.all_to_all(scan_state, "dp", split_axis=1, concat_axis=0, tiled=True),
        lax.all_to_all(key_cache, "dp", split_axis=1, concat_axis=0, tiled=True),
        lax.all_to_all(value_cache, "dp", split_axis=1, concat_axis=0, tiled=True),
    )
    parent_taps, parent_state, parent_keys, parent_values = (
        lax.all_to_all(
            choose_rows(arrived[0], state_picks), "dp", split_axis=0, concat_axis=1, tiled=True
        ),
        lax.all_to_all(
            choose_rows(arrived[1], state_picks), "dp", split_axis=0, concat_axis=1, tiled=True
        ),
        lax.all_to_all(
            choose_rows(arrived[2], cache_picks), "dp", split_axis=0, concat_axis=1, tiled=True
        ),
        lax.all_to_all(
            choose_rows(arrived[3], cache_picks), "dp", split_axis=0, concat_axis=1, tiled=True
        ),
    )
    children = lax.dynamic_slice_in_dim(prompt_parents, my_index * beam_slots, beam_slots, 0)
    parent_length = jnp.take_along_axis(local_lengths, children, axis=0)
    queries = query.reshape((beam_slots, cache_prompts, kv_local, group_size, HEAD_DIM))
    new_keys = fresh_key.reshape((beam_slots, cache_prompts, kv_local, HEAD_DIM))
    new_values = fresh_value.reshape((beam_slots, cache_prompts, kv_local, HEAD_DIM))
    keys_split = parent_keys.reshape((beam_slots, cache_prompts, cache_length, kv_local, HEAD_DIM))
    values_split = parent_values.reshape(
        (beam_slots, cache_prompts, cache_length, kv_local, HEAD_DIM)
    )
    scores = (
        jnp.einsum("rpkgd,rptkd->rpkgt", queries, keys_split, preferred_element_type=jnp.float32)
        * score_scale
    )
    live_mask = positions[None, None, None, None, :] < parent_length[:, :, None, None, None]
    fresh_score = (
        jnp.einsum("rpkgd,rpkd->rpkg", queries, new_keys, preferred_element_type=jnp.float32)
        * score_scale
    )
    row_max = jnp.maximum(jnp.max(jnp.where(live_mask, scores, big_negative), axis=-1), fresh_score)
    weights = jnp.where(live_mask, jnp.exp(scores - row_max[..., None]), 0.0)
    fresh_weight = jnp.exp(fresh_score - row_max)
    row_total = jnp.sum(weights, axis=-1) + fresh_weight
    weights_half = (weights / row_total[..., None]).astype(jnp.bfloat16)
    fresh_half = (fresh_weight / row_total).astype(jnp.bfloat16)
    attended = jnp.einsum(
        "rpkgt,rptkd->rpkgd", weights_half, values_split, preferred_element_type=jnp.float32
    )
    attended = (
        attended
        + fresh_half.astype(jnp.float32)[..., None]
        * new_values.astype(jnp.float32)[:, :, :, None, :]
    )
    attention_output = attended.reshape((beam_slots, cache_prompts, heads_local * HEAD_DIM)).astype(
        jnp.bfloat16
    )
    window = jnp.concatenate([parent_taps, token_input[:, :, None, :]], axis=2)
    conv_output = jax.nn.silu(
        jnp.sum(window.astype(jnp.float32) * conv_weight.astype(jnp.float32), axis=2) + conv_bias
    )
    conv_half = conv_output.astype(jnp.bfloat16)
    partial_sums = jnp.einsum(
        "bpc,cr->bpr", conv_half, select_weight, preferred_element_type=jnp.float32
    )
    projected = lax.psum(partial_sums, ("tensor", "sub"))
    rank_size = step_gain.shape[0]
    state_size = decay_log.shape[0]
    step_raw = projected[..., :rank_size]
    state_input = projected[..., rank_size : rank_size + state_size]
    state_readout = projected[..., rank_size + state_size :]
    step_norm = (
        step_raw
        * lax.rsqrt(jnp.mean(step_raw * step_raw, axis=-1, keepdims=True) + 1e-06)
        * step_gain
    ).astype(jnp.bfloat16)
    step_size = jax.nn.softplus(
        jnp.einsum("bpr,rc->bpc", step_norm, step_weight, preferred_element_type=jnp.float32)
        + step_bias
    )
    decay_factor = jnp.exp(-step_size[:, :, None, :] * jnp.exp(decay_log)[None, None])
    state_next = (
        decay_factor * parent_state.astype(jnp.float32)
        + step_size[:, :, None, :] * state_input[..., None] * conv_output[:, :, None, :]
    )
    readout = jnp.sum(state_readout[..., None] * state_next, axis=2) + skip_gain * conv_output
    mamba_output = (readout * jax.nn.silu(gate_input.astype(jnp.float32))).astype(jnp.bfloat16)
    return (state_next.astype(jnp.bfloat16), window[:, :, 1:, :], mamba_output, attention_output)


def body(*arrays):
    token_input, parents = arrays[0], arrays[-1]
    sizes = (lax.axis_size("dp"), token_input.shape[0], token_input.shape[1], parents.shape[1])
    paired = lax.axis_size("tensor") == 2 and lax.axis_size("sub") == 2
    if sizes == (4, 4, 8, 16) and paired:
        return quick_body(*arrays)
    return general_body(*arrays)


def solution(mesh):
    placed = (
        P("dp", "groups", ("tensor", "sub")),
        P("dp", "groups", ("tensor", "sub")),
        P("dp", "groups", None, ("tensor", "sub")),
        P("dp", "groups", None, ("tensor", "sub")),
        P(None, ("tensor", "sub")),
        P(("tensor", "sub")),
        P(("tensor", "sub"), None),
        P(),
        P(None, ("tensor", "sub")),
        P(("tensor", "sub")),
        P(None, ("tensor", "sub")),
        P(("tensor", "sub")),
        P("dp", ("groups", "sub"), "tensor"),
        P("dp", ("groups", "sub"), "tensor"),
        P("dp", ("groups", "sub"), "tensor"),
        P("dp", ("groups", "sub"), None, "tensor"),
        P("dp", ("groups", "sub"), None, "tensor"),
        P(None, "groups"),
        P("groups", None),
    )
    return jax.shard_map(
        body,
        mesh=mesh,
        in_specs=placed,
        out_specs=(
            P("dp", "groups", None, ("tensor", "sub")),
            P("dp", "groups", None, ("tensor", "sub")),
            P("dp", "groups", ("tensor", "sub")),
            P("dp", ("groups", "sub"), "tensor"),
        ),
        check_vma=False,
    )
```

```python
import functools

import jax
import jax.numpy as jnp
import numpy as np
from jax import lax
from jax.experimental import pallas as pl
from jax.experimental.pallas import tpu as pltpu
from jax.sharding import PartitionSpec as P

HEADS = 64
KV_HEADS = 8
HEAD_DIM = 128
GROUP = HEADS // KV_HEADS

big_negative = -1e30

TIERS = ((16, 12, 12), (18, 13, 13), (20, 15, 15), (24, 18, 18), (32, 32, 32))
VMEM = 48 * 1024 * 1024
TINY = pl.CostEstimate(flops=1000, bytes_accessed=1000, transcendentals=0)


def pairs(mask):
    return [(i, i ^ mask) for i in range(4)]


def send(x, mask):
    return lax.ppermute(x, "dp", pairs(mask))


def plan_kernel(me_ref, parents_ref, plan):
    me = me_ref[0]
    row = lax.broadcasted_iota(jnp.int32, (128, 1), 0)
    owner = row // 32
    child_owner = lax.broadcasted_iota(jnp.int32, (128, 16), 1) // 4
    prompt = lax.broadcasted_iota(jnp.int32, (128, 8), 1)
    spread = jnp.where(lax.broadcasted_iota(jnp.int32, (128, 8), 0) % 8 == prompt, 1.0, 0.0)
    tiled = jnp.dot(
        spread, parents_ref[...].astype(jnp.float32), preferred_element_type=jnp.float32
    ).astype(jnp.int32)
    equal = tiled == row // 8
    child_lane = lax.broadcasted_iota(jnp.int32, (128, 16), 1)
    chosen = child_lane == me * 4 + row // 8
    target = jnp.sum(jnp.where(chosen, tiled, 0), axis=1, keepdims=True) * 8 + row % 8

    def wanted(mask):
        hit = equal & (child_owner == (owner ^ mask))
        return jnp.max(jnp.where(hit, 1.0, 0.0), axis=1, keepdims=True)

    passed = wanted(3)
    crossing = wanted(2) * (1.0 - passed)
    beside = wanted(1)
    lane = lax.broadcasted_iota(jnp.int32, (128, 128), 1)
    down = lax.broadcasted_iota(jnp.int32, (128, 128), 0)
    flags = jnp.where(
        lane == 0, passed, jnp.where(lane == 1, crossing, jnp.where(lane == 2, beside, 0.0))
    )
    same = lane // 32 == down // 32
    before = jnp.where(same & (lane < down), 1.0, 0.0)
    ahead = jnp.dot(before, flags, preferred_element_type=jnp.float32)
    totals = jnp.dot(jnp.where(same, 1.0, 0.0), flags, preferred_element_type=jnp.float32)
    x_slot = jnp.where(
        passed > 0.0,
        ahead[:, 0:1],
        jnp.where(crossing > 0.0, totals[:, 0:1] + ahead[:, 1:2], -1.0),
    ).astype(jnp.int32)
    o_slot = jnp.where(beside > 0.0, ahead[:, 2:3], -1.0).astype(jnp.int32)
    mine = owner == me
    local = row % 32

    def listing(slot_of):
        hit = (slot_of == lane) & mine
        return jnp.max(jnp.where(hit, local, -1), axis=0, keepdims=True)

    place = jnp.where(
        mine,
        local,
        jnp.where(
            owner == (me ^ 2),
            32 + x_slot,
            jnp.where(owner == (me ^ 1), 64 + o_slot, 96 + x_slot),
        ),
    )
    place_across = jnp.sum(jnp.where(lane == down, place, 0), axis=0, keepdims=True)
    code_down = jnp.sum(jnp.where(lane == target, place_across, 0), axis=1, keepdims=True)
    code = jnp.sum(jnp.where(lane == down, code_down, 0), axis=0, keepdims=True)
    x_most = jnp.max(totals[:, 0:1] + totals[:, 1:2], axis=0, keepdims=True)
    f_most = jnp.max(totals[:, 0:1], axis=0, keepdims=True)
    o_most = jnp.max(totals[:, 2:3], axis=0, keepdims=True)
    tier = jnp.zeros((1, 1), jnp.int32)
    for c, f, o in TIERS[:-1]:
        over = (x_most > float(c)) | (f_most > float(f)) | (o_most > float(o))
        tier += jnp.where(over, 1, 0)
    handed = jnp.full((1, 1), TIERS[-1][1], jnp.int32)
    for index in range(len(TIERS) - 1):
        handed = jnp.where(tier == index, TIERS[index][1], handed)
    child = row < 32
    late = child & ((code_down >= 96) | ((code_down >= 32 + handed) & (code_down < 64)))
    early = child & jnp.logical_not(late)
    groups = jnp.where(
        lane == 0, jnp.where(early, 1.0, 0.0), jnp.where(lane == 1, jnp.where(late, 1.0, 0.0), 0.0)
    )
    earlier = jnp.where(lane < down, 1.0, 0.0)
    position = jnp.dot(earlier, groups, preferred_element_type=jnp.float32).astype(jnp.int32)
    amount = jnp.sum(groups, axis=0, keepdims=True).astype(jnp.int32)

    def members(index, group):
        hit = (position[:, index : index + 1] == lane) & group
        return jnp.max(jnp.where(hit, row, -1), axis=0, keepdims=True)

    plan[0:1, :] = listing(x_slot)
    plan[1:2, :] = listing(o_slot)
    plan[2:3, :] = code
    plan[3:4, :] = jnp.broadcast_to(tier, (1, 128))
    plan[4:5, :] = members(0, early)
    plan[5:6, :] = members(1, late)
    plan[6:7, :] = amount
    plan[7:8, :] = jnp.ones((1, 128), jnp.int32)


def make_plan(parents, me):
    return pl.pallas_call(
        plan_kernel,
        in_specs=[pl.BlockSpec(memory_space=pltpu.SMEM), pl.BlockSpec(memory_space=pltpu.VMEM)],
        out_specs=pl.BlockSpec(memory_space=pltpu.VMEM),
        out_shape=jax.ShapeDtypeStruct((8, 128), jnp.int32),
        name="plan",
    )(me.reshape(1), parents)


def attend_kernel(heads, q_ref, k_ref, v_ref, lo_ref, hi_ref, *outs):
    lo = jnp.concatenate([lo_ref[0]] * GROUP, axis=0)
    hi = jnp.concatenate([hi_ref[0]] * GROUP, axis=0)
    beams, _, length, _ = k_ref.shape
    keys = beams * length
    column = lax.broadcasted_iota(jnp.int32, (16 * GROUP, keys), 1)
    live = (column >= lo) & (column < hi)
    local = (hi > lo).astype(jnp.float32)
    scale = HEAD_DIM**-0.5
    width = GROUP * HEAD_DIM
    key_base = heads * width
    value_base = key_base + heads * HEAD_DIM
    for k in range(heads):
        q = jnp.concatenate(
            [
                q_ref[0, :, k * width + g * HEAD_DIM : k * width + (g + 1) * HEAD_DIM]
                for g in range(GROUP)
            ],
            axis=0,
        )
        head = slice(k * HEAD_DIM, (k + 1) * HEAD_DIM)
        keys_here = k_ref[:, 0, :, head].reshape(keys, HEAD_DIM)
        values_here = v_ref[:, 0, :, head].reshape(keys, HEAD_DIM)
        new_key = q_ref[0, :, key_base + k * HEAD_DIM : key_base + (k + 1) * HEAD_DIM]
        new_value = q_ref[0, :, value_base + k * HEAD_DIM : value_base + (k + 1) * HEAD_DIM]
        scores = (
            lax.dot_general(
                q, keys_here, (((1,), (1,)), ((), ())), preferred_element_type=jnp.float32
            )
            * scale
        )
        new_keys = jnp.concatenate([new_key.astype(jnp.float32)] * GROUP, axis=0)
        new_values = jnp.concatenate([new_value.astype(jnp.float32)] * GROUP, axis=0)
        fresh = jnp.sum(q.astype(jnp.float32) * new_keys, axis=1, keepdims=True) * scale
        scores = jnp.where(live, scores, big_negative)
        top = jnp.maximum(jnp.max(scores, axis=1, keepdims=True), fresh)
        weights = jnp.exp(scores - top)
        fresh_weight = jnp.exp(fresh - top)
        share = 1.0 / (jnp.sum(weights, axis=1, keepdims=True) + fresh_weight)
        half = (weights * share).astype(jnp.bfloat16)
        fresh_half = (fresh_weight * share).astype(jnp.bfloat16).astype(jnp.float32)
        mixed = jnp.dot(half, values_here, preferred_element_type=jnp.float32)
        mixed = jnp.where(local > 0.0, mixed + fresh_half * new_values, 0.0).astype(jnp.bfloat16)
        for block in range(4):
            out = outs[block % 2]
            for g in range(GROUP):
                out[block // 2, 0, :, k * width + g * HEAD_DIM : k * width + (g + 1) * HEAD_DIM] = mixed[
                    g * 16 + 4 * block : g * 16 + 4 * block + 4
                ]


def attend(queries, keys, values, lo, hi):
    prompts, children, width = queries.shape
    beams, _, length, depth = keys.shape
    heads = depth // HEAD_DIM
    wide = heads * GROUP * HEAD_DIM
    spec = pl.BlockSpec((beams, 1, length, depth), lambda p: (0, p, 0, 0))
    bound = pl.BlockSpec((1, children, 1), lambda p: (p, 0, 0))
    return pl.pallas_call(
        functools.partial(attend_kernel, heads),
        grid=(prompts,),
        in_specs=[pl.BlockSpec((1, children, width), lambda p: (p, 0, 0)), spec, spec, bound, bound],
        out_specs=[pl.BlockSpec((2, 1, 4, wide), lambda p: (0, p, 0, 0))] * 2,
        out_shape=[jax.ShapeDtypeStruct((2, prompts, 4, wide), jnp.bfloat16)] * 2,
        compiler_params=pltpu.CompilerParams(vmem_limit_bytes=VMEM),
        cost_estimate=TINY,
        name="attend",
    )(queries, keys, values, lo, hi)


def one_hot(column, width):
    lane = lax.broadcasted_iota(jnp.int32, (column.shape[0], width), 1)
    return (lane == column).astype(jnp.bfloat16)


def pick(column, table):
    return jnp.dot(one_hot(column, table.shape[0]), table, preferred_element_type=jnp.float32)


def pack_taps_kernel(*refs):
    half = len(refs) // 2
    taps = refs[half][...]
    for column, out in zip(refs[:half], refs[half + 1 :]):
        out[...] = pick(column[...], taps).astype(jnp.bfloat16)


def pack_taps(tier, plan, taps):
    c, f, o = tier
    width = taps.shape[1]
    listings = [plan[0, :c], plan[1, :o]] + ([plan[0, :f]] if c > f else [])
    columns = [
        jnp.concatenate(
            [jnp.where(base >= 0, base // 8 * 24 + 8 * k + base % 8, -1) for k in range(3)]
        )[:, None]
        for base in listings
    ]
    vmem = pl.BlockSpec(memory_space=pltpu.VMEM)
    outs = pl.pallas_call(
        pack_taps_kernel,
        in_specs=[vmem] * (len(columns) + 1),
        out_specs=[vmem] * len(columns),
        out_shape=[jax.ShapeDtypeStruct((x.shape[0], width), jnp.bfloat16) for x in columns],
        compiler_params=pltpu.CompilerParams(vmem_limit_bytes=VMEM),
        cost_estimate=TINY,
        name="pack_taps",
    )(*columns, taps)
    return outs if c > f else (*outs, outs[0])


def pack_kernel(tier, plan, state, *rest):
    c, f, o = tier
    sems = rest[-1]
    xa, out = rest[0], rest[-2]

    def copies(which, first, count, target, base):
        def start(s, _):
            row = jnp.maximum(plan[which, first + s], 0)
            pltpu.make_async_copy(state.at[row], target.at[s], sems.at[base + s]).start()
            return 0

        lax.fori_loop(0, count, start, 0)

    copies(0, 0, f, xa, 0)
    copies(1, 0, o, out, c)
    if c > f:
        copies(0, f, c - f, rest[1], f)

    def finish(s, _):
        pltpu.make_async_copy(state.at[0], xa.at[0], sems.at[s]).wait()
        return 0

    lax.fori_loop(0, c + o, finish, 0)


def pack(tier, plan, state):
    c, f, o = tier
    rows = [f] + ([c - f] if c > f else []) + [o]
    vmem = pl.BlockSpec(memory_space=pltpu.VMEM)
    anywhere = pl.BlockSpec(memory_space=pl.ANY)
    outs = pl.pallas_call(
        functools.partial(pack_kernel, tier),
        in_specs=[pl.BlockSpec(memory_space=pltpu.SMEM), vmem],
        out_specs=[anywhere] * len(rows),
        out_shape=[jax.ShapeDtypeStruct((n,) + state.shape[1:], jnp.bfloat16) for n in rows],
        scratch_shapes=[pltpu.SemaphoreType.DMA((c + o,))],
        compiler_params=pltpu.CompilerParams(vmem_limit_bytes=VMEM),
        cost_estimate=TINY,
        name="pack",
    )(plan, state)
    if c == f:
        return outs[0], None, outs[1]
    return outs


def conv_kernel(code, token, weight, bias, select, taps, *rest):
    *tables, conv_out, next_taps, partial = rest
    count = token.shape[0]
    code = code[...]
    tap = lax.broadcasted_iota(jnp.int32, (3 * count, 1), 0) // count

    def part(base, table):
        size = table.shape[0] // 3
        slot = code - base
        inside = (slot >= 0) & (slot < size)
        return pick(jnp.where(inside, slot + tap * size, -1), table[...])

    window = pick(jnp.where(code < 32, code // 8 * 24 + tap * 8 + code % 8, -1), taps[...])
    for index, table in enumerate(tables):
        window += part(32 * (index + 1), table)
    fresh = token[...]
    for start in range(0, count, 8):
        for k, source in enumerate((window[count : 2 * count], window[2 * count :], fresh)):
            next_taps[3 * start + 8 * k : 3 * start + 8 * k + 8, :] = source[
                start : start + 8
            ].astype(jnp.bfloat16)
    w = weight[...].astype(jnp.float32)
    total = window[:count] * w[0:1]
    total += window[count : 2 * count] * w[1:2]
    total += window[2 * count :] * w[2:3]
    total += fresh.astype(jnp.float32) * w[3:4]
    v = total + bias[...]
    conv = v / (1.0 + jnp.exp(-v))
    conv_out[...] = conv
    partial[...] = lax.dot_general(
        conv.astype(jnp.bfloat16),
        select[...],
        (((1,), (1,)), ((), ())),
        preferred_element_type=jnp.float32,
    )


def convolve(code, token, weight, bias, select, taps, tables):
    count, width = token.shape
    vmem = pl.BlockSpec(memory_space=pltpu.VMEM)
    return pl.pallas_call(
        conv_kernel,
        in_specs=[vmem] * (6 + len(tables)),
        out_specs=[vmem] * 3,
        out_shape=[
            jax.ShapeDtypeStruct((count, width), jnp.float32),
            jax.ShapeDtypeStruct((3 * count, width), jnp.bfloat16),
            jax.ShapeDtypeStruct((count, select.shape[0]), jnp.float32),
        ],
        compiler_params=pltpu.CompilerParams(vmem_limit_bytes=VMEM),
        cost_estimate=TINY,
        name="convolve",
    )(code, token, weight, bias, select, taps, *tables)


def step_kernel(projected, across, gain, weight, bias, step, b_wide, c_wide):
    rank = gain.shape[1]
    raw = projected[:, :rank]
    mean = jnp.mean(raw * raw, axis=1, keepdims=True)
    norm = (raw * lax.rsqrt(mean + 1e-06) * gain[...]).astype(jnp.bfloat16)
    v = jnp.dot(norm, weight[...], preferred_element_type=jnp.float32) + bias[...]
    step[...] = jnp.maximum(v, 0.0) + jnp.log1p(jnp.exp(-jnp.abs(v)))
    states = b_wide.shape[1]
    for r in range(b_wide.shape[0]):
        b_wide[r] = jnp.broadcast_to(across[:states, r : r + 1], b_wide.shape[1:])
        c_wide[r] = jnp.broadcast_to(across[states:, r : r + 1], c_wide.shape[1:])


def step_sizes(projected, gain, weight, bias):
    count, width = projected.shape[0], weight.shape[1]
    rank = gain.shape[1]
    across = projected[:, rank:].T
    states = across.shape[0] // 2
    vmem = pl.BlockSpec(memory_space=pltpu.VMEM)
    wide = jax.ShapeDtypeStruct((count, states, 128), jnp.float32)
    return pl.pallas_call(
        step_kernel,
        in_specs=[vmem] * 5,
        out_specs=[vmem] * 3,
        out_shape=[jax.ShapeDtypeStruct((count, width), jnp.float32), wide, wide],
        compiler_params=pltpu.CompilerParams(vmem_limit_bytes=VMEM),
        cost_estimate=TINY,
        name="step_sizes",
    )(projected, across, gain, weight, bias)


def advance(plan, which, starts, step, conv, rates, b_in, c_in, held, done, lines, next_state, sems):
    total = plan[6, which]
    in_sems, out_sems = sems

    def begin(n, _):
        r = plan[4 + which, n]
        where = plan[2, r]
        for condition, source, base in starts:

            @pl.when(condition(where))
            def _(source=source, base=base):
                pltpu.make_async_copy(source.at[where - base], held.at[n], in_sems.at[n]).start()

        return 0

    lax.fori_loop(0, total, begin, 0)
    def work(n, _):
        r = plan[4 + which, n]
        pltpu.make_async_copy(next_state.at[0], held.at[n], in_sems.at[n]).wait()
        b = b_in[r]
        c_out = c_in[r]
        sizes = step[pl.ds(r, 1), :]
        gains = sizes * conv[pl.ds(r, 1), :]
        readouts = []
        for first in range(0, step.shape[1], 128):
            part = slice(first, first + 128)
            state = held[n, :, part].astype(jnp.float32)
            new = jnp.exp(-sizes[:, part] * rates[:, part]) * state + gains[:, part] * b
            done[n, :, part] = new.astype(jnp.bfloat16)
            readouts.append(jnp.sum(c_out * new, axis=0, keepdims=True))
        lines[pl.ds(r, 1), :] = lines[pl.ds(r, 1), :] + jnp.concatenate(readouts, axis=1)
        pltpu.make_async_copy(done.at[n], next_state.at[r], out_sems.at[n]).start()
        return 0

    lax.fori_loop(0, total, work, 0)

    def finish(n, _):
        pltpu.make_async_copy(done.at[n], next_state.at[0], out_sems.at[n]).wait()
        return 0

    lax.fori_loop(0, total, finish, 0)


def early_kernel(
    tier, plan, step, conv, decay_log, skip, gate, b_in, c_in, local, xa, beside, next_state, lines, opened, held, done, rates, *sems
):
    f = tier[1]
    rates[...] = jnp.exp(decay_log[...])
    lines[...] = skip[...] * conv[...]
    gates = gate[...].astype(jnp.float32)
    opened[...] = gates / (1.0 + jnp.exp(-gates))
    starts = (
        (lambda w: w < 32, local, 0),
        (lambda w: (w >= 32) & (w < 32 + f), xa, 32),
        (lambda w: (w >= 64) & (w < 96), beside, 64),
    )
    advance(plan, 0, starts, step, conv, rates, b_in, c_in, held, done, lines, next_state, sems)


def late_kernel(
    tier, has_xb, plan, step, conv, decay_log, b_in, c_in, lines_in, opened, *rest
):
    f = tier[1]
    sources, rest = rest[: 2 if has_xb else 1], rest[2 if has_xb else 1 :]
    _, next_state, output, held, done, rates, lines, *sems = rest
    rates[...] = jnp.exp(decay_log[...])
    lines[...] = lines_in[...]
    starts = [(lambda w: w >= 96, sources[-1], 96)]
    if has_xb:
        starts.append((lambda w: w < 96, sources[0], 32 + f))
    advance(plan, 1, starts, step, conv, rates, b_in, c_in, held, done, lines, next_state, sems)
    output[...] = (lines[...] * opened[...]).astype(jnp.bfloat16)


def scan_scratch(count, states, width):
    return [
        pltpu.VMEM((count, states, width), jnp.bfloat16),
        pltpu.VMEM((count, states, width), jnp.bfloat16),
        pltpu.VMEM((states, width), jnp.float32),
    ], [pltpu.SemaphoreType.DMA((count,)), pltpu.SemaphoreType.DMA((count,))]


def early(tier, plan, step, conv, decay_log, skip, gate, b_in, c_in, local, xa, beside):
    count, width = step.shape
    states = decay_log.shape[0]
    vmem = pl.BlockSpec(memory_space=pltpu.VMEM)
    anywhere = pl.BlockSpec(memory_space=pl.ANY)
    arrays, sems = scan_scratch(count, states, width)
    return pl.pallas_call(
        functools.partial(early_kernel, tier),
        in_specs=[pl.BlockSpec(memory_space=pltpu.SMEM)] + [vmem] * 7 + [anywhere] * 3,
        out_specs=[anywhere, vmem, vmem],
        out_shape=[
            jax.ShapeDtypeStruct((count, states, width), jnp.bfloat16),
            jax.ShapeDtypeStruct((count, width), jnp.float32),
            jax.ShapeDtypeStruct((count, width), jnp.float32),
        ],
        scratch_shapes=arrays + sems,
        compiler_params=pltpu.CompilerParams(vmem_limit_bytes=VMEM),
        cost_estimate=TINY,
        name="early",
    )(plan, step, conv, decay_log, skip, gate, b_in, c_in, local, xa, beside)


def late(tier, plan, step, conv, decay_log, b_in, c_in, lines, opened, buffers, next_state):
    count, width = step.shape
    states = decay_log.shape[0]
    vmem = pl.BlockSpec(memory_space=pltpu.VMEM)
    anywhere = pl.BlockSpec(memory_space=pl.ANY)
    arrays, sems = scan_scratch(count, states, width)
    return pl.pallas_call(
        functools.partial(late_kernel, tier, len(buffers) == 2),
        in_specs=[pl.BlockSpec(memory_space=pltpu.SMEM)]
        + [vmem] * 7
        + [anywhere] * (len(buffers) + 1),
        out_specs=[anywhere, vmem],
        out_shape=[
            jax.ShapeDtypeStruct((count, states, width), jnp.bfloat16),
            jax.ShapeDtypeStruct((count, width), jnp.bfloat16),
        ],
        scratch_shapes=arrays + [pltpu.VMEM((count, width), jnp.float32)] + sems,
        input_output_aliases={8 + len(buffers): 0},
        compiler_params=pltpu.CompilerParams(vmem_limit_bytes=VMEM),
        cost_estimate=TINY,
        name="late",
    )(plan, step, conv, decay_log, b_in, c_in, lines, opened, *buffers, next_state)


def across_chips(x):
    others = [lax.ppermute(x, ("tensor", "sub"), pairs(mask)) for mask in (1, 2, 3)]
    return x, *others


def quick_body(
    token_input,
    gate_input,
    conv_taps,
    scan_state,
    conv_weight,
    conv_bias,
    select_weight,
    step_gain,
    step_weight,
    step_bias,
    decay_log,
    skip_gain,
    query,
    fresh_key,
    fresh_value,
    key_cache,
    value_cache,
    cache_lengths,
    parents,
):
    me = lax.axis_index("dp")
    beams, prompts, width = token_input.shape
    states, rank = decay_log.shape[0], step_gain.shape[0]
    count = beams * prompts
    cache_prompts, length = key_cache.shape[1], key_cache.shape[2]
    first = lax.axis_index("sub") * cache_prompts

    plan = make_plan(parents, me)
    asked = jnp.concatenate([query, fresh_key, fresh_value], axis=2)
    asked = [asked, send(asked, 1), send(asked, 2)]
    taps = conv_taps.transpose(0, 2, 1, 3).reshape(3 * count, width)
    state = scan_state.reshape(count, states, width)

    def bounds():
        here = lax.dynamic_slice_in_dim(parents, first, cache_prompts, 0)
        lengths = lax.dynamic_slice_in_dim(cache_lengths, first, cache_prompts, 1)
        related = jnp.concatenate(
            [lax.dynamic_slice_in_dim(here, (me ^ mask) * beams, beams, 1) for mask in range(4)], axis=1
        )
        live = jnp.sum(
            jnp.where(
                related[:, :, None] == np.arange(16)[None, None, :], lengths.T[:, None, :], 0
            ),
            axis=2,
        )
        local = related // beams == me
        lo = jnp.where(local, (related % beams) * length, 0)
        hi = jnp.where(local, lo + live, 0)
        return lo[:, :, None], hi[:, :, None]

    def middle(plan, taps, tables, asked):
        conv, next_taps, partial = convolve(
            jnp.tile(plan[2, :count], 3)[:, None],
            token_input.reshape(count, width),
            conv_weight,
            conv_bias[None],
            select_weight.T,
            taps,
            tables,
        )
        shares = across_chips(partial)
        queries = jnp.concatenate(asked, axis=0).transpose(1, 0, 2)
        outs = attend(queries, key_cache, value_cache, *bounds())
        shares, outs = lax.optimization_barrier((shares, outs))
        beside = send(outs[1], 1)
        projected = (shares[0] + shares[1]) + (shares[2] + shares[3])
        step, b_in, c_in = step_sizes(projected, step_gain[None], step_weight, step_bias[None])
        back = outs[0] + beside
        return lax.optimization_barrier((conv, next_taps, step, b_in, c_in, back))

    def skipped(plan, taps, tables, asked):
        shapes = jax.eval_shape(middle, plan, taps, tables, asked)
        return jax.tree.map(lambda x: jnp.zeros(x.shape, x.dtype), shapes)

    def run(limits):
        c, f, o = limits

        def branch(plan, taps, state, asked):
            asked = [*asked, send(asked[2], 1)]
            tx, to, tf = pack_taps(limits, plan, taps)
            tables = [send(tx, 2), send(to, 1), send(tf, 3)]
            xa, xb, near = pack(limits, plan, state)
            near = send(near, 1)
            xa, tables, asked = lax.optimization_barrier((xa, tables, asked))
            xa = send(xa, 2)
            conv, next_taps, step, b_in, c_in, back = lax.cond(
                plan[7, 0] == 1, middle, skipped, plan, taps, tables, asked
            )
            second = [back] if xb is None else [back, xb]
            xa, near, step, *second = lax.optimization_barrier((xa, near, step, *second))
            passed = send(xa, 1)
            buffers = [passed] if xb is None else [send(second[1], 2), passed]
            attention = (second[0][0] + send(second[0][1], 2)).transpose(1, 0, 2)
            next_state, lines, opened = early(
                limits,
                plan,
                step,
                conv,
                decay_log,
                skip_gain[None],
                gate_input.reshape(count, width),
                b_in,
                c_in,
                state,
                xa,
                near,
            )
            next_state, output = late(
                limits, plan, step, conv, decay_log, b_in, c_in, lines, opened, buffers, next_state
            )
            return next_state, next_taps, output, attention

        return branch

    next_state, next_taps, output, attention = lax.switch(
        plan[3, 0],
        [run(limits) for limits in TIERS],
        plan,
        taps,
        state,
        asked,
    )
    return (
        next_state.reshape(beams, prompts, states, width),
        next_taps.reshape(beams, 3, prompts, width).transpose(0, 2, 1, 3),
        output.reshape(beams, prompts, width),
        attention,
    )


def choose_rows(array, picks):
    index = picks.reshape(picks.shape + (1,) * (array.ndim - 2))
    return jnp.take_along_axis(array, index, axis=0)


def parent_rows(parents, first, count):
    return lax.dynamic_slice_in_dim(parents, first, count, 0).T


def general_body(
    token_input,
    gate_input,
    conv_taps,
    scan_state,
    conv_weight,
    conv_bias,
    select_weight,
    step_gain,
    step_weight,
    step_bias,
    decay_log,
    skip_gain,
    query,
    fresh_key,
    fresh_value,
    key_cache,
    value_cache,
    cache_lengths,
    parents,
):
    group_width = lax.axis_size("dp")
    my_index = lax.axis_index("dp")
    sub_index = lax.axis_index("sub")
    beam_slots = token_input.shape[0]
    prompt_count = token_input.shape[1]
    prompt_share = prompt_count // group_width
    cache_prompts = key_cache.shape[1]
    cache_share = cache_prompts // group_width
    cache_base = sub_index * cache_prompts
    cache_length = key_cache.shape[2]
    group_size = HEADS // KV_HEADS
    score_scale = HEAD_DIM ** (-0.5)
    heads_local = query.shape[2] // HEAD_DIM
    kv_local = fresh_key.shape[2] // HEAD_DIM
    state_picks = parent_rows(parents, my_index * prompt_share, prompt_share)
    cache_picks = parent_rows(parents, cache_base + my_index * cache_share, cache_share)
    local_lengths = lax.dynamic_slice_in_dim(cache_lengths, cache_base, cache_prompts, 1)
    prompt_parents = parent_rows(parents, cache_base, cache_prompts)
    positions = jnp.arange(cache_length, dtype=jnp.int32)
    arrived = (
        lax.all_to_all(conv_taps, "dp", split_axis=1, concat_axis=0, tiled=True),
        lax.all_to_all(scan_state, "dp", split_axis=1, concat_axis=0, tiled=True),
        lax.all_to_all(key_cache, "dp", split_axis=1, concat_axis=0, tiled=True),
        lax.all_to_all(value_cache, "dp", split_axis=1, concat_axis=0, tiled=True),
    )
    parent_taps, parent_state, parent_keys, parent_values = (
        lax.all_to_all(
            choose_rows(arrived[0], state_picks), "dp", split_axis=0, concat_axis=1, tiled=True
        ),
        lax.all_to_all(
            choose_rows(arrived[1], state_picks), "dp", split_axis=0, concat_axis=1, tiled=True
        ),
        lax.all_to_all(
            choose_rows(arrived[2], cache_picks), "dp", split_axis=0, concat_axis=1, tiled=True
        ),
        lax.all_to_all(
            choose_rows(arrived[3], cache_picks), "dp", split_axis=0, concat_axis=1, tiled=True
        ),
    )
    children = lax.dynamic_slice_in_dim(prompt_parents, my_index * beam_slots, beam_slots, 0)
    parent_length = jnp.take_along_axis(local_lengths, children, axis=0)
    queries = query.reshape((beam_slots, cache_prompts, kv_local, group_size, HEAD_DIM))
    new_keys = fresh_key.reshape((beam_slots, cache_prompts, kv_local, HEAD_DIM))
    new_values = fresh_value.reshape((beam_slots, cache_prompts, kv_local, HEAD_DIM))
    keys_split = parent_keys.reshape((beam_slots, cache_prompts, cache_length, kv_local, HEAD_DIM))
    values_split = parent_values.reshape(
        (beam_slots, cache_prompts, cache_length, kv_local, HEAD_DIM)
    )
    scores = (
        jnp.einsum("rpkgd,rptkd->rpkgt", queries, keys_split, preferred_element_type=jnp.float32)
        * score_scale
    )
    live_mask = positions[None, None, None, None, :] < parent_length[:, :, None, None, None]
    fresh_score = (
        jnp.einsum("rpkgd,rpkd->rpkg", queries, new_keys, preferred_element_type=jnp.float32)
        * score_scale
    )
    row_max = jnp.maximum(jnp.max(jnp.where(live_mask, scores, big_negative), axis=-1), fresh_score)
    weights = jnp.where(live_mask, jnp.exp(scores - row_max[..., None]), 0.0)
    fresh_weight = jnp.exp(fresh_score - row_max)
    row_total = jnp.sum(weights, axis=-1) + fresh_weight
    weights_half = (weights / row_total[..., None]).astype(jnp.bfloat16)
    fresh_half = (fresh_weight / row_total).astype(jnp.bfloat16)
    attended = jnp.einsum(
        "rpkgt,rptkd->rpkgd", weights_half, values_split, preferred_element_type=jnp.float32
    )
    attended = (
        attended
        + fresh_half.astype(jnp.float32)[..., None]
        * new_values.astype(jnp.float32)[:, :, :, None, :]
    )
    attention_output = attended.reshape((beam_slots, cache_prompts, heads_local * HEAD_DIM)).astype(
        jnp.bfloat16
    )
    window = jnp.concatenate([parent_taps, token_input[:, :, None, :]], axis=2)
    conv_output = jax.nn.silu(
        jnp.sum(window.astype(jnp.float32) * conv_weight.astype(jnp.float32), axis=2) + conv_bias
    )
    conv_half = conv_output.astype(jnp.bfloat16)
    partial_sums = jnp.einsum(
        "bpc,cr->bpr", conv_half, select_weight, preferred_element_type=jnp.float32
    )
    projected = lax.psum(partial_sums, ("tensor", "sub"))
    rank_size = step_gain.shape[0]
    state_size = decay_log.shape[0]
    step_raw = projected[..., :rank_size]
    state_input = projected[..., rank_size : rank_size + state_size]
    state_readout = projected[..., rank_size + state_size :]
    step_norm = (
        step_raw
        * lax.rsqrt(jnp.mean(step_raw * step_raw, axis=-1, keepdims=True) + 1e-06)
        * step_gain
    ).astype(jnp.bfloat16)
    step_size = jax.nn.softplus(
        jnp.einsum("bpr,rc->bpc", step_norm, step_weight, preferred_element_type=jnp.float32)
        + step_bias
    )
    decay_factor = jnp.exp(-step_size[:, :, None, :] * jnp.exp(decay_log)[None, None])
    state_next = (
        decay_factor * parent_state.astype(jnp.float32)
        + step_size[:, :, None, :] * state_input[..., None] * conv_output[:, :, None, :]
    )
    readout = jnp.sum(state_readout[..., None] * state_next, axis=2) + skip_gain * conv_output
    mamba_output = (readout * jax.nn.silu(gate_input.astype(jnp.float32))).astype(jnp.bfloat16)
    return (state_next.astype(jnp.bfloat16), window[:, :, 1:, :], mamba_output, attention_output)


def body(*arrays):
    token_input, parents = arrays[0], arrays[-1]
    sizes = (lax.axis_size("dp"), token_input.shape[0], token_input.shape[1], parents.shape[1])
    paired = lax.axis_size("tensor") == 2 and lax.axis_size("sub") == 2
    if sizes == (4, 4, 8, 16) and paired:
        return quick_body(*arrays)
    return general_body(*arrays)


def solution(mesh):
    placed = (
        P("dp", "groups", ("tensor", "sub")),
        P("dp", "groups", ("tensor", "sub")),
        P("dp", "groups", None, ("tensor", "sub")),
        P("dp", "groups", None, ("tensor", "sub")),
        P(None, ("tensor", "sub")),
        P(("tensor", "sub")),
        P(("tensor", "sub"), None),
        P(),
        P(None, ("tensor", "sub")),
        P(("tensor", "sub")),
        P(None, ("tensor", "sub")),
        P(("tensor", "sub")),
        P("dp", ("groups", "sub"), "tensor"),
        P("dp", ("groups", "sub"), "tensor"),
        P("dp", ("groups", "sub"), "tensor"),
        P("dp", ("groups", "sub"), None, "tensor"),
        P("dp", ("groups", "sub"), None, "tensor"),
        P(None, "groups"),
        P("groups", None),
    )
    return jax.shard_map(
        body,
        mesh=mesh,
        in_specs=placed,
        out_specs=(
            P("dp", "groups", None, ("tensor", "sub")),
            P("dp", "groups", None, ("tensor", "sub")),
            P("dp", "groups", ("tensor", "sub")),
            P("dp", ("groups", "sub"), "tensor"),
        ),
        check_vma=False,
    )
```

```python
import functools

import jax
import jax.numpy as jnp
import numpy as np
from jax import lax
from jax.experimental import pallas as pl
from jax.experimental.pallas import tpu as pltpu
from jax.sharding import PartitionSpec as P

HEADS = 64
KV_HEADS = 8
HEAD_DIM = 128
GROUP = HEADS // KV_HEADS

big_negative = -1e30

TIERS = ((16, 12, 12), (18, 13, 13), (20, 15, 15), (24, 18, 18), (32, 32, 32))
VMEM = 48 * 1024 * 1024
TINY = pl.CostEstimate(flops=1000, bytes_accessed=1000, transcendentals=0)


def pairs(mask):
    return [(i, i ^ mask) for i in range(4)]


def send(x, mask):
    return lax.ppermute(x, "dp", pairs(mask))


def plan_kernel(me_ref, parents_ref, plan):
    me = me_ref[0]
    row = lax.broadcasted_iota(jnp.int32, (128, 1), 0)
    owner = row // 32
    child_owner = lax.broadcasted_iota(jnp.int32, (128, 16), 1) // 4
    prompt = lax.broadcasted_iota(jnp.int32, (128, 8), 1)
    spread = jnp.where(lax.broadcasted_iota(jnp.int32, (128, 8), 0) % 8 == prompt, 1.0, 0.0)
    tiled = jnp.dot(
        spread, parents_ref[...].astype(jnp.float32), preferred_element_type=jnp.float32
    ).astype(jnp.int32)
    equal = tiled == row // 8
    child_lane = lax.broadcasted_iota(jnp.int32, (128, 16), 1)
    chosen = child_lane == me * 4 + row // 8
    target = jnp.sum(jnp.where(chosen, tiled, 0), axis=1, keepdims=True) * 8 + row % 8

    def wanted(mask):
        hit = equal & (child_owner == (owner ^ mask))
        return jnp.max(jnp.where(hit, 1.0, 0.0), axis=1, keepdims=True)

    passed = wanted(3)
    crossing = wanted(2) * (1.0 - passed)
    beside = wanted(1)
    lane = lax.broadcasted_iota(jnp.int32, (128, 128), 1)
    down = lax.broadcasted_iota(jnp.int32, (128, 128), 0)
    flags = jnp.where(
        lane == 0, passed, jnp.where(lane == 1, crossing, jnp.where(lane == 2, beside, 0.0))
    )
    same = lane // 32 == down // 32
    before = jnp.where(same & (lane < down), 1.0, 0.0)
    ahead = jnp.dot(before, flags, preferred_element_type=jnp.float32)
    totals = jnp.dot(jnp.where(same, 1.0, 0.0), flags, preferred_element_type=jnp.float32)
    x_slot = jnp.where(
        passed > 0.0,
        ahead[:, 0:1],
        jnp.where(crossing > 0.0, totals[:, 0:1] + ahead[:, 1:2], -1.0),
    ).astype(jnp.int32)
    o_slot = jnp.where(beside > 0.0, ahead[:, 2:3], -1.0).astype(jnp.int32)
    mine = owner == me
    local = row % 32

    def listing(slot_of):
        hit = (slot_of == lane) & mine
        return jnp.max(jnp.where(hit, local, -1), axis=0, keepdims=True)

    place = jnp.where(
        mine,
        local,
        jnp.where(
            owner == (me ^ 2),
            32 + x_slot,
            jnp.where(owner == (me ^ 1), 64 + o_slot, 96 + x_slot),
        ),
    )
    place_across = jnp.sum(jnp.where(lane == down, place, 0), axis=0, keepdims=True)
    code_down = jnp.sum(jnp.where(lane == target, place_across, 0), axis=1, keepdims=True)
    code = jnp.sum(jnp.where(lane == down, code_down, 0), axis=0, keepdims=True)
    x_most = jnp.max(totals[:, 0:1] + totals[:, 1:2], axis=0, keepdims=True)
    f_most = jnp.max(totals[:, 0:1], axis=0, keepdims=True)
    o_most = jnp.max(totals[:, 2:3], axis=0, keepdims=True)
    tier = jnp.zeros((1, 1), jnp.int32)
    for c, f, o in TIERS[:-1]:
        over = (x_most > float(c)) | (f_most > float(f)) | (o_most > float(o))
        tier += jnp.where(over, 1, 0)
    handed = jnp.full((1, 1), TIERS[-1][1], jnp.int32)
    for index in range(len(TIERS) - 1):
        handed = jnp.where(tier == index, TIERS[index][1], handed)
    child = row < 32
    late = child & ((code_down >= 96) | ((code_down >= 32 + handed) & (code_down < 64)))
    early = child & jnp.logical_not(late)
    groups = jnp.where(
        lane == 0, jnp.where(early, 1.0, 0.0), jnp.where(lane == 1, jnp.where(late, 1.0, 0.0), 0.0)
    )
    earlier = jnp.where(lane < down, 1.0, 0.0)
    position = jnp.dot(earlier, groups, preferred_element_type=jnp.float32).astype(jnp.int32)
    amount = jnp.sum(groups, axis=0, keepdims=True).astype(jnp.int32)

    def members(index, group):
        hit = (position[:, index : index + 1] == lane) & group
        return jnp.max(jnp.where(hit, row, -1), axis=0, keepdims=True)

    plan[0:1, :] = listing(x_slot)
    plan[1:2, :] = listing(o_slot)
    plan[2:3, :] = code
    plan[3:4, :] = jnp.broadcast_to(tier, (1, 128))
    plan[4:5, :] = members(0, early)
    plan[5:6, :] = members(1, late)
    plan[6:7, :] = amount
    plan[7:8, :] = jnp.ones((1, 128), jnp.int32)


def make_plan(parents, me):
    return pl.pallas_call(
        plan_kernel,
        in_specs=[pl.BlockSpec(memory_space=pltpu.SMEM), pl.BlockSpec(memory_space=pltpu.VMEM)],
        out_specs=pl.BlockSpec(memory_space=pltpu.VMEM),
        out_shape=jax.ShapeDtypeStruct((8, 128), jnp.int32),
        name="plan",
    )(me.reshape(1), parents)


def attend_kernel(heads, q_ref, k_ref, v_ref, lo_ref, hi_ref, *outs):
    lo = jnp.concatenate([lo_ref[0]] * GROUP, axis=0)
    hi = jnp.concatenate([hi_ref[0]] * GROUP, axis=0)
    beams, _, length, _ = k_ref.shape
    keys = beams * length
    column = lax.broadcasted_iota(jnp.int32, (16 * GROUP, keys), 1)
    live = (column >= lo) & (column < hi)
    local = (hi > lo).astype(jnp.float32)
    scale = HEAD_DIM**-0.5
    width = GROUP * HEAD_DIM
    key_base = heads * width
    value_base = key_base + heads * HEAD_DIM
    for k in range(heads):
        q = jnp.concatenate(
            [
                q_ref[0, :, k * width + g * HEAD_DIM : k * width + (g + 1) * HEAD_DIM]
                for g in range(GROUP)
            ],
            axis=0,
        )
        head = slice(k * HEAD_DIM, (k + 1) * HEAD_DIM)
        keys_here = k_ref[:, 0, :, head].reshape(keys, HEAD_DIM)
        values_here = v_ref[:, 0, :, head].reshape(keys, HEAD_DIM)
        new_key = q_ref[0, :, key_base + k * HEAD_DIM : key_base + (k + 1) * HEAD_DIM]
        new_value = q_ref[0, :, value_base + k * HEAD_DIM : value_base + (k + 1) * HEAD_DIM]
        scores = (
            lax.dot_general(
                q, keys_here, (((1,), (1,)), ((), ())), preferred_element_type=jnp.float32
            )
            * scale
        )
        new_keys = jnp.concatenate([new_key.astype(jnp.float32)] * GROUP, axis=0)
        new_values = jnp.concatenate([new_value.astype(jnp.float32)] * GROUP, axis=0)
        fresh = jnp.sum(q.astype(jnp.float32) * new_keys, axis=1, keepdims=True) * scale
        scores = jnp.where(live, scores, big_negative)
        top = jnp.maximum(jnp.max(scores, axis=1, keepdims=True), fresh)
        weights = jnp.exp(scores - top)
        fresh_weight = jnp.exp(fresh - top)
        share = 1.0 / (jnp.sum(weights, axis=1, keepdims=True) + fresh_weight)
        half = (weights * share).astype(jnp.bfloat16)
        fresh_half = (fresh_weight * share).astype(jnp.bfloat16).astype(jnp.float32)
        mixed = jnp.dot(half, values_here, preferred_element_type=jnp.float32)
        mixed = jnp.where(local > 0.0, mixed + fresh_half * new_values, 0.0).astype(jnp.bfloat16)
        for block in range(4):
            out = outs[block % 2]
            for g in range(GROUP):
                out[block // 2, 0, :, k * width + g * HEAD_DIM : k * width + (g + 1) * HEAD_DIM] = mixed[
                    g * 16 + 4 * block : g * 16 + 4 * block + 4
                ]


def attend(queries, keys, values, lo, hi):
    prompts, children, width = queries.shape
    beams, _, length, depth = keys.shape
    heads = depth // HEAD_DIM
    wide = heads * GROUP * HEAD_DIM
    spec = pl.BlockSpec((beams, 1, length, depth), lambda p: (0, p, 0, 0))
    bound = pl.BlockSpec((1, children, 1), lambda p: (p, 0, 0))
    return pl.pallas_call(
        functools.partial(attend_kernel, heads),
        grid=(prompts,),
        in_specs=[pl.BlockSpec((1, children, width), lambda p: (p, 0, 0)), spec, spec, bound, bound],
        out_specs=[pl.BlockSpec((2, 1, 4, wide), lambda p: (0, p, 0, 0))] * 2,
        out_shape=[jax.ShapeDtypeStruct((2, prompts, 4, wide), jnp.bfloat16)] * 2,
        compiler_params=pltpu.CompilerParams(vmem_limit_bytes=VMEM),
        cost_estimate=TINY,
        name="attend",
    )(queries, keys, values, lo, hi)


def one_hot(column, width):
    lane = lax.broadcasted_iota(jnp.int32, (column.shape[0], width), 1)
    return (lane == column).astype(jnp.bfloat16)


def pick(column, table):
    return jnp.dot(one_hot(column, table.shape[0]), table, preferred_element_type=jnp.float32)


def pack_taps_kernel(*refs):
    half = len(refs) // 2
    taps = refs[half][...]
    for column, out in zip(refs[:half], refs[half + 1 :]):
        out[...] = pick(column[...], taps).astype(jnp.bfloat16)


def pack_taps(tier, plan, taps):
    c, f, o = tier
    width = taps.shape[1]
    listings = [plan[0, :c], plan[1, :o]] + ([plan[0, :f]] if c > f else [])
    columns = [
        jnp.concatenate(
            [jnp.where(base >= 0, base // 8 * 24 + 8 * k + base % 8, -1) for k in range(3)]
        )[:, None]
        for base in listings
    ]
    vmem = pl.BlockSpec(memory_space=pltpu.VMEM)
    outs = pl.pallas_call(
        pack_taps_kernel,
        in_specs=[vmem] * (len(columns) + 1),
        out_specs=[vmem] * len(columns),
        out_shape=[jax.ShapeDtypeStruct((x.shape[0], width), jnp.bfloat16) for x in columns],
        compiler_params=pltpu.CompilerParams(vmem_limit_bytes=VMEM),
        cost_estimate=TINY,
        name="pack_taps",
    )(*columns, taps)
    return outs if c > f else (*outs, outs[0])


def pack_kernel(tier, plan, state, *rest):
    c, f, o = tier
    sems = rest[-1]
    xa, out = rest[0], rest[-2]

    def copies(which, first, count, target, base):
        def start(s, _):
            row = jnp.maximum(plan[which, first + s], 0)
            pltpu.make_async_copy(state.at[row], target.at[s], sems.at[base + s]).start()
            return 0

        lax.fori_loop(0, count, start, 0)

    copies(0, 0, f, xa, 0)
    copies(1, 0, o, out, c)
    if c > f:
        copies(0, f, c - f, rest[1], f)

    def finish(s, _):
        pltpu.make_async_copy(state.at[0], xa.at[0], sems.at[s]).wait()
        return 0

    lax.fori_loop(0, c + o, finish, 0)


def pack(tier, plan, state):
    c, f, o = tier
    rows = [f] + ([c - f] if c > f else []) + [o]
    vmem = pl.BlockSpec(memory_space=pltpu.VMEM)
    anywhere = pl.BlockSpec(memory_space=pl.ANY)
    outs = pl.pallas_call(
        functools.partial(pack_kernel, tier),
        in_specs=[pl.BlockSpec(memory_space=pltpu.SMEM), vmem],
        out_specs=[anywhere] * len(rows),
        out_shape=[jax.ShapeDtypeStruct((n,) + state.shape[1:], jnp.bfloat16) for n in rows],
        scratch_shapes=[pltpu.SemaphoreType.DMA((c + o,))],
        compiler_params=pltpu.CompilerParams(vmem_limit_bytes=VMEM),
        cost_estimate=TINY,
        name="pack",
    )(plan, state)
    if c == f:
        return outs[0], None, outs[1]
    return outs


def conv_kernel(code, token, weight, bias, select, taps, *rest):
    *tables, conv_out, next_taps, partial = rest
    count = token.shape[0]
    code = code[...]
    tap = lax.broadcasted_iota(jnp.int32, (3 * count, 1), 0) // count

    def part(base, table):
        size = table.shape[0] // 3
        slot = code - base
        inside = (slot >= 0) & (slot < size)
        return pick(jnp.where(inside, slot + tap * size, -1), table[...])

    window = pick(jnp.where(code < 32, code // 8 * 24 + tap * 8 + code % 8, -1), taps[...])
    for index, table in enumerate(tables):
        window += part(32 * (index + 1), table)
    fresh = token[...]
    for start in range(0, count, 8):
        for k, source in enumerate((window[count : 2 * count], window[2 * count :], fresh)):
            next_taps[3 * start + 8 * k : 3 * start + 8 * k + 8, :] = source[
                start : start + 8
            ].astype(jnp.bfloat16)
    w = weight[...].astype(jnp.float32)
    total = window[:count] * w[0:1]
    total += window[count : 2 * count] * w[1:2]
    total += window[2 * count :] * w[2:3]
    total += fresh.astype(jnp.float32) * w[3:4]
    v = total + bias[...]
    conv = v / (1.0 + jnp.exp(-v))
    conv_out[...] = conv
    partial[...] = lax.dot_general(
        conv.astype(jnp.bfloat16),
        select[...],
        (((1,), (1,)), ((), ())),
        preferred_element_type=jnp.float32,
    )


def convolve(code, token, weight, bias, select, taps, tables):
    count, width = token.shape
    vmem = pl.BlockSpec(memory_space=pltpu.VMEM)
    return pl.pallas_call(
        conv_kernel,
        in_specs=[vmem] * (6 + len(tables)),
        out_specs=[vmem] * 3,
        out_shape=[
            jax.ShapeDtypeStruct((count, width), jnp.float32),
            jax.ShapeDtypeStruct((3 * count, width), jnp.bfloat16),
            jax.ShapeDtypeStruct((count, select.shape[0]), jnp.float32),
        ],
        compiler_params=pltpu.CompilerParams(vmem_limit_bytes=VMEM),
        cost_estimate=TINY,
        name="convolve",
    )(code, token, weight, bias, select, taps, *tables)


def step_kernel(projected, across, gain, weight, bias, step, b_wide, c_wide):
    rank = gain.shape[1]
    raw = projected[:, :rank]
    mean = jnp.mean(raw * raw, axis=1, keepdims=True)
    norm = (raw * lax.rsqrt(mean + 1e-06) * gain[...]).astype(jnp.bfloat16)
    v = jnp.dot(norm, weight[...], preferred_element_type=jnp.float32) + bias[...]
    step[...] = jnp.maximum(v, 0.0) + jnp.log1p(jnp.exp(-jnp.abs(v)))
    states = b_wide.shape[1]
    for r in range(b_wide.shape[0]):
        b_wide[r] = jnp.broadcast_to(across[:states, r : r + 1], b_wide.shape[1:])
        c_wide[r] = jnp.broadcast_to(across[states:, r : r + 1], c_wide.shape[1:])


def step_sizes(projected, gain, weight, bias):
    count, width = projected.shape[0], weight.shape[1]
    rank = gain.shape[1]
    across = projected[:, rank:].T
    states = across.shape[0] // 2
    vmem = pl.BlockSpec(memory_space=pltpu.VMEM)
    wide = jax.ShapeDtypeStruct((count, states, 128), jnp.float32)
    return pl.pallas_call(
        step_kernel,
        in_specs=[vmem] * 5,
        out_specs=[vmem] * 3,
        out_shape=[jax.ShapeDtypeStruct((count, width), jnp.float32), wide, wide],
        compiler_params=pltpu.CompilerParams(vmem_limit_bytes=VMEM),
        cost_estimate=TINY,
        name="step_sizes",
    )(projected, across, gain, weight, bias)


def advance(plan, which, starts, step, conv, rates, b_in, c_in, held, done, lines, next_state, sems):
    total = plan[6, which]
    in_sems, out_sems = sems

    def begin(n, _):
        r = plan[4 + which, n]
        where = plan[2, r]
        for condition, source, base in starts:

            @pl.when(condition(where))
            def _(source=source, base=base):
                pltpu.make_async_copy(source.at[where - base], held.at[n], in_sems.at[n]).start()

        return 0

    lax.fori_loop(0, total, begin, 0)
    def one(n):
        valid = n < total
        r = jnp.maximum(plan[4 + which, n], 0)

        @pl.when(valid)
        def _():
            pltpu.make_async_copy(next_state.at[0], held.at[n], in_sems.at[n]).wait()

        b = b_in[r]
        c_out = c_in[r]
        sizes = step[pl.ds(r, 1), :]
        gains = sizes * conv[pl.ds(r, 1), :]
        readouts = []
        for first in range(0, step.shape[1], 128):
            part = slice(first, first + 128)
            state = held[n, :, part].astype(jnp.float32)
            new = jnp.exp(-sizes[:, part] * rates[:, part]) * state + gains[:, part] * b
            done[n, :, part] = new.astype(jnp.bfloat16)
            readouts.append(jnp.sum(c_out * new, axis=0, keepdims=True))
        return valid, r, jnp.concatenate(readouts, axis=1)

    def work(m, _):
        rows = [one(2 * m), one(2 * m + 1)]
        for offset, (valid, r, readout) in enumerate(rows):
            n = 2 * m + offset

            @pl.when(valid)
            def _(r=r, n=n, readout=readout):
                lines[pl.ds(r, 1), :] = lines[pl.ds(r, 1), :] + readout
                pltpu.make_async_copy(done.at[n], next_state.at[r], out_sems.at[n]).start()

        return 0

    lax.fori_loop(0, (total + 1) // 2, work, 0)

    def finish(n, _):
        pltpu.make_async_copy(done.at[n], next_state.at[0], out_sems.at[n]).wait()
        return 0

    lax.fori_loop(0, total, finish, 0)


def early_kernel(
    tier, plan, step, conv, decay_log, skip, gate, b_in, c_in, local, xa, beside, next_state, lines, opened, held, done, rates, *sems
):
    f = tier[1]
    rates[...] = jnp.exp(decay_log[...])
    lines[...] = skip[...] * conv[...]
    gates = gate[...].astype(jnp.float32)
    opened[...] = gates / (1.0 + jnp.exp(-gates))
    starts = (
        (lambda w: w < 32, local, 0),
        (lambda w: (w >= 32) & (w < 32 + f), xa, 32),
        (lambda w: (w >= 64) & (w < 96), beside, 64),
    )
    advance(plan, 0, starts, step, conv, rates, b_in, c_in, held, done, lines, next_state, sems)


def late_kernel(
    tier, has_xb, plan, step, conv, decay_log, b_in, c_in, lines_in, opened, *rest
):
    f = tier[1]
    sources, rest = rest[: 2 if has_xb else 1], rest[2 if has_xb else 1 :]
    _, next_state, output, held, done, rates, lines, *sems = rest
    rates[...] = jnp.exp(decay_log[...])
    lines[...] = lines_in[...]
    starts = [(lambda w: w >= 96, sources[-1], 96)]
    if has_xb:
        starts.append((lambda w: w < 96, sources[0], 32 + f))
    advance(plan, 1, starts, step, conv, rates, b_in, c_in, held, done, lines, next_state, sems)
    output[...] = (lines[...] * opened[...]).astype(jnp.bfloat16)


def scan_scratch(count, states, width):
    return [
        pltpu.VMEM((count, states, width), jnp.bfloat16),
        pltpu.VMEM((count, states, width), jnp.bfloat16),
        pltpu.VMEM((states, width), jnp.float32),
    ], [pltpu.SemaphoreType.DMA((count,)), pltpu.SemaphoreType.DMA((count,))]


def early(tier, plan, step, conv, decay_log, skip, gate, b_in, c_in, local, xa, beside):
    count, width = step.shape
    states = decay_log.shape[0]
    vmem = pl.BlockSpec(memory_space=pltpu.VMEM)
    anywhere = pl.BlockSpec(memory_space=pl.ANY)
    arrays, sems = scan_scratch(count, states, width)
    return pl.pallas_call(
        functools.partial(early_kernel, tier),
        in_specs=[pl.BlockSpec(memory_space=pltpu.SMEM)] + [vmem] * 7 + [anywhere] * 3,
        out_specs=[anywhere, vmem, vmem],
        out_shape=[
            jax.ShapeDtypeStruct((count, states, width), jnp.bfloat16),
            jax.ShapeDtypeStruct((count, width), jnp.float32),
            jax.ShapeDtypeStruct((count, width), jnp.float32),
        ],
        scratch_shapes=arrays + sems,
        compiler_params=pltpu.CompilerParams(vmem_limit_bytes=VMEM),
        cost_estimate=TINY,
        name="early",
    )(plan, step, conv, decay_log, skip, gate, b_in, c_in, local, xa, beside)


def late(tier, plan, step, conv, decay_log, b_in, c_in, lines, opened, buffers, next_state):
    count, width = step.shape
    states = decay_log.shape[0]
    vmem = pl.BlockSpec(memory_space=pltpu.VMEM)
    anywhere = pl.BlockSpec(memory_space=pl.ANY)
    arrays, sems = scan_scratch(count, states, width)
    return pl.pallas_call(
        functools.partial(late_kernel, tier, len(buffers) == 2),
        in_specs=[pl.BlockSpec(memory_space=pltpu.SMEM)]
        + [vmem] * 7
        + [anywhere] * (len(buffers) + 1),
        out_specs=[anywhere, vmem],
        out_shape=[
            jax.ShapeDtypeStruct((count, states, width), jnp.bfloat16),
            jax.ShapeDtypeStruct((count, width), jnp.bfloat16),
        ],
        scratch_shapes=arrays + [pltpu.VMEM((count, width), jnp.float32)] + sems,
        input_output_aliases={8 + len(buffers): 0},
        compiler_params=pltpu.CompilerParams(vmem_limit_bytes=VMEM),
        cost_estimate=TINY,
        name="late",
    )(plan, step, conv, decay_log, b_in, c_in, lines, opened, *buffers, next_state)


def across_chips(x):
    others = [lax.ppermute(x, ("tensor", "sub"), pairs(mask)) for mask in (1, 2, 3)]
    return x, *others


def quick_body(
    token_input,
    gate_input,
    conv_taps,
    scan_state,
    conv_weight,
    conv_bias,
    select_weight,
    step_gain,
    step_weight,
    step_bias,
    decay_log,
    skip_gain,
    query,
    fresh_key,
    fresh_value,
    key_cache,
    value_cache,
    cache_lengths,
    parents,
):
    me = lax.axis_index("dp")
    beams, prompts, width = token_input.shape
    states, rank = decay_log.shape[0], step_gain.shape[0]
    count = beams * prompts
    cache_prompts, length = key_cache.shape[1], key_cache.shape[2]
    first = lax.axis_index("sub") * cache_prompts

    plan = make_plan(parents, me)
    asked = jnp.concatenate([query, fresh_key, fresh_value], axis=2)
    asked = [asked, send(asked, 1), send(asked, 2)]
    taps = conv_taps.transpose(0, 2, 1, 3).reshape(3 * count, width)
    state = scan_state.reshape(count, states, width)

    def bounds():
        here = lax.dynamic_slice_in_dim(parents, first, cache_prompts, 0)
        lengths = lax.dynamic_slice_in_dim(cache_lengths, first, cache_prompts, 1)
        related = jnp.concatenate(
            [lax.dynamic_slice_in_dim(here, (me ^ mask) * beams, beams, 1) for mask in range(4)], axis=1
        )
        live = jnp.sum(
            jnp.where(
                related[:, :, None] == np.arange(16)[None, None, :], lengths.T[:, None, :], 0
            ),
            axis=2,
        )
        local = related // beams == me
        lo = jnp.where(local, (related % beams) * length, 0)
        hi = jnp.where(local, lo + live, 0)
        return lo[:, :, None], hi[:, :, None]

    def middle(plan, taps, tables, asked):
        conv, next_taps, partial = convolve(
            jnp.tile(plan[2, :count], 3)[:, None],
            token_input.reshape(count, width),
            conv_weight,
            conv_bias[None],
            select_weight.T,
            taps,
            tables,
        )
        shares = across_chips(partial)
        queries = jnp.concatenate(asked, axis=0).transpose(1, 0, 2)
        outs = attend(queries, key_cache, value_cache, *bounds())
        shares, outs = lax.optimization_barrier((shares, outs))
        beside = send(outs[1], 1)
        projected = (shares[0] + shares[1]) + (shares[2] + shares[3])
        step, b_in, c_in = step_sizes(projected, step_gain[None], step_weight, step_bias[None])
        back = outs[0][1] + beside[1]
        return lax.optimization_barrier(
            (conv, next_taps, step, b_in, c_in, back, outs[0][0], beside[0])
        )

    def skipped(plan, taps, tables, asked):
        shapes = jax.eval_shape(middle, plan, taps, tables, asked)
        return jax.tree.map(lambda x: jnp.zeros(x.shape, x.dtype), shapes)

    def run(limits):
        c, f, o = limits

        def branch(plan, taps, state, asked):
            asked = [*asked, send(asked[2], 1)]
            tx, to, tf = pack_taps(limits, plan, taps)
            tables = [send(tx, 2), send(to, 1), send(tf, 3)]
            xa, xb, near = pack(limits, plan, state)
            near = send(near, 1)
            xa, tables, asked = lax.optimization_barrier((xa, tables, asked))
            xa = send(xa, 2)
            conv, next_taps, step, b_in, c_in, back, own, beside = lax.cond(
                plan[7, 0] == 1, middle, skipped, plan, taps, tables, asked
            )
            second = [back] if xb is None else [back, xb]
            xa, near, step, *second = lax.optimization_barrier((xa, near, step, *second))
            passed = send(xa, 1)
            buffers = [passed] if xb is None else [send(second[1], 2), passed]
            attention = (own + beside + send(second[0], 2)).transpose(1, 0, 2)
            next_state, lines, opened = early(
                limits,
                plan,
                step,
                conv,
                decay_log,
                skip_gain[None],
                gate_input.reshape(count, width),
                b_in,
                c_in,
                state,
                xa,
                near,
            )
            next_state, output = late(
                limits, plan, step, conv, decay_log, b_in, c_in, lines, opened, buffers, next_state
            )
            return next_state, next_taps, output, attention

        return branch

    next_state, next_taps, output, attention = lax.switch(
        plan[3, 0],
        [run(limits) for limits in TIERS],
        plan,
        taps,
        state,
        asked,
    )
    return (
        next_state.reshape(beams, prompts, states, width),
        next_taps.reshape(beams, 3, prompts, width).transpose(0, 2, 1, 3),
        output.reshape(beams, prompts, width),
        attention,
    )


def choose_rows(array, picks):
    index = picks.reshape(picks.shape + (1,) * (array.ndim - 2))
    return jnp.take_along_axis(array, index, axis=0)


def parent_rows(parents, first, count):
    return lax.dynamic_slice_in_dim(parents, first, count, 0).T


def general_body(
    token_input,
    gate_input,
    conv_taps,
    scan_state,
    conv_weight,
    conv_bias,
    select_weight,
    step_gain,
    step_weight,
    step_bias,
    decay_log,
    skip_gain,
    query,
    fresh_key,
    fresh_value,
    key_cache,
    value_cache,
    cache_lengths,
    parents,
):
    group_width = lax.axis_size("dp")
    my_index = lax.axis_index("dp")
    sub_index = lax.axis_index("sub")
    beam_slots = token_input.shape[0]
    prompt_count = token_input.shape[1]
    prompt_share = prompt_count // group_width
    cache_prompts = key_cache.shape[1]
    cache_share = cache_prompts // group_width
    cache_base = sub_index * cache_prompts
    cache_length = key_cache.shape[2]
    group_size = HEADS // KV_HEADS
    score_scale = HEAD_DIM ** (-0.5)
    heads_local = query.shape[2] // HEAD_DIM
    kv_local = fresh_key.shape[2] // HEAD_DIM
    state_picks = parent_rows(parents, my_index * prompt_share, prompt_share)
    cache_picks = parent_rows(parents, cache_base + my_index * cache_share, cache_share)
    local_lengths = lax.dynamic_slice_in_dim(cache_lengths, cache_base, cache_prompts, 1)
    prompt_parents = parent_rows(parents, cache_base, cache_prompts)
    positions = jnp.arange(cache_length, dtype=jnp.int32)
    arrived = (
        lax.all_to_all(conv_taps, "dp", split_axis=1, concat_axis=0, tiled=True),
        lax.all_to_all(scan_state, "dp", split_axis=1, concat_axis=0, tiled=True),
        lax.all_to_all(key_cache, "dp", split_axis=1, concat_axis=0, tiled=True),
        lax.all_to_all(value_cache, "dp", split_axis=1, concat_axis=0, tiled=True),
    )
    parent_taps, parent_state, parent_keys, parent_values = (
        lax.all_to_all(
            choose_rows(arrived[0], state_picks), "dp", split_axis=0, concat_axis=1, tiled=True
        ),
        lax.all_to_all(
            choose_rows(arrived[1], state_picks), "dp", split_axis=0, concat_axis=1, tiled=True
        ),
        lax.all_to_all(
            choose_rows(arrived[2], cache_picks), "dp", split_axis=0, concat_axis=1, tiled=True
        ),
        lax.all_to_all(
            choose_rows(arrived[3], cache_picks), "dp", split_axis=0, concat_axis=1, tiled=True
        ),
    )
    children = lax.dynamic_slice_in_dim(prompt_parents, my_index * beam_slots, beam_slots, 0)
    parent_length = jnp.take_along_axis(local_lengths, children, axis=0)
    queries = query.reshape((beam_slots, cache_prompts, kv_local, group_size, HEAD_DIM))
    new_keys = fresh_key.reshape((beam_slots, cache_prompts, kv_local, HEAD_DIM))
    new_values = fresh_value.reshape((beam_slots, cache_prompts, kv_local, HEAD_DIM))
    keys_split = parent_keys.reshape((beam_slots, cache_prompts, cache_length, kv_local, HEAD_DIM))
    values_split = parent_values.reshape(
        (beam_slots, cache_prompts, cache_length, kv_local, HEAD_DIM)
    )
    scores = (
        jnp.einsum("rpkgd,rptkd->rpkgt", queries, keys_split, preferred_element_type=jnp.float32)
        * score_scale
    )
    live_mask = positions[None, None, None, None, :] < parent_length[:, :, None, None, None]
    fresh_score = (
        jnp.einsum("rpkgd,rpkd->rpkg", queries, new_keys, preferred_element_type=jnp.float32)
        * score_scale
    )
    row_max = jnp.maximum(jnp.max(jnp.where(live_mask, scores, big_negative), axis=-1), fresh_score)
    weights = jnp.where(live_mask, jnp.exp(scores - row_max[..., None]), 0.0)
    fresh_weight = jnp.exp(fresh_score - row_max)
    row_total = jnp.sum(weights, axis=-1) + fresh_weight
    weights_half = (weights / row_total[..., None]).astype(jnp.bfloat16)
    fresh_half = (fresh_weight / row_total).astype(jnp.bfloat16)
    attended = jnp.einsum(
        "rpkgt,rptkd->rpkgd", weights_half, values_split, preferred_element_type=jnp.float32
    )
    attended = (
        attended
        + fresh_half.astype(jnp.float32)[..., None]
        * new_values.astype(jnp.float32)[:, :, :, None, :]
    )
    attention_output = attended.reshape((beam_slots, cache_prompts, heads_local * HEAD_DIM)).astype(
        jnp.bfloat16
    )
    window = jnp.concatenate([parent_taps, token_input[:, :, None, :]], axis=2)
    conv_output = jax.nn.silu(
        jnp.sum(window.astype(jnp.float32) * conv_weight.astype(jnp.float32), axis=2) + conv_bias
    )
    conv_half = conv_output.astype(jnp.bfloat16)
    partial_sums = jnp.einsum(
        "bpc,cr->bpr", conv_half, select_weight, preferred_element_type=jnp.float32
    )
    projected = lax.psum(partial_sums, ("tensor", "sub"))
    rank_size = step_gain.shape[0]
    state_size = decay_log.shape[0]
    step_raw = projected[..., :rank_size]
    state_input = projected[..., rank_size : rank_size + state_size]
    state_readout = projected[..., rank_size + state_size :]
    step_norm = (
        step_raw
        * lax.rsqrt(jnp.mean(step_raw * step_raw, axis=-1, keepdims=True) + 1e-06)
        * step_gain
    ).astype(jnp.bfloat16)
    step_size = jax.nn.softplus(
        jnp.einsum("bpr,rc->bpc", step_norm, step_weight, preferred_element_type=jnp.float32)
        + step_bias
    )
    decay_factor = jnp.exp(-step_size[:, :, None, :] * jnp.exp(decay_log)[None, None])
    state_next = (
        decay_factor * parent_state.astype(jnp.float32)
        + step_size[:, :, None, :] * state_input[..., None] * conv_output[:, :, None, :]
    )
    readout = jnp.sum(state_readout[..., None] * state_next, axis=2) + skip_gain * conv_output
    mamba_output = (readout * jax.nn.silu(gate_input.astype(jnp.float32))).astype(jnp.bfloat16)
    return (state_next.astype(jnp.bfloat16), window[:, :, 1:, :], mamba_output, attention_output)


def body(*arrays):
    token_input, parents = arrays[0], arrays[-1]
    sizes = (lax.axis_size("dp"), token_input.shape[0], token_input.shape[1], parents.shape[1])
    paired = lax.axis_size("tensor") == 2 and lax.axis_size("sub") == 2
    if sizes == (4, 4, 8, 16) and paired:
        return quick_body(*arrays)
    return general_body(*arrays)


def solution(mesh):
    placed = (
        P("dp", "groups", ("tensor", "sub")),
        P("dp", "groups", ("tensor", "sub")),
        P("dp", "groups", None, ("tensor", "sub")),
        P("dp", "groups", None, ("tensor", "sub")),
        P(None, ("tensor", "sub")),
        P(("tensor", "sub")),
        P(("tensor", "sub"), None),
        P(),
        P(None, ("tensor", "sub")),
        P(("tensor", "sub")),
        P(None, ("tensor", "sub")),
        P(("tensor", "sub")),
        P("dp", ("groups", "sub"), "tensor"),
        P("dp", ("groups", "sub"), "tensor"),
        P("dp", ("groups", "sub"), "tensor"),
        P("dp", ("groups", "sub"), None, "tensor"),
        P("dp", ("groups", "sub"), None, "tensor"),
        P(None, "groups"),
        P("groups", None),
    )
    return jax.shard_map(
        body,
        mesh=mesh,
        in_specs=placed,
        out_specs=(
            P("dp", "groups", None, ("tensor", "sub")),
            P("dp", "groups", None, ("tensor", "sub")),
            P("dp", "groups", ("tensor", "sub")),
            P("dp", ("groups", "sub"), "tensor"),
        ),
        check_vma=False,
    )
```

```python
import functools

import jax
import jax.numpy as jnp
import numpy as np
from jax import lax
from jax.experimental import pallas as pl
from jax.experimental.pallas import tpu as pltpu
from jax.sharding import PartitionSpec as P

HEADS = 64
KV_HEADS = 8
HEAD_DIM = 128
GROUP = HEADS // KV_HEADS

big_negative = -1e30

TIERS = ((16, 12, 12), (18, 13, 13), (20, 15, 15), (23, 17, 18), (32, 32, 32))
VMEM = 48 * 1024 * 1024
TINY = pl.CostEstimate(flops=1000, bytes_accessed=1000, transcendentals=0)


def pairs(mask):
    return [(i, i ^ mask) for i in range(4)]


def send(x, mask):
    return lax.ppermute(x, "dp", pairs(mask))


def plan_kernel(me_ref, parents_ref, plan):
    me = me_ref[0]
    row = lax.broadcasted_iota(jnp.int32, (128, 1), 0)
    owner = row // 32
    child_owner = lax.broadcasted_iota(jnp.int32, (128, 16), 1) // 4
    prompt = lax.broadcasted_iota(jnp.int32, (128, 8), 1)
    spread = jnp.where(lax.broadcasted_iota(jnp.int32, (128, 8), 0) % 8 == prompt, 1.0, 0.0)
    tiled = jnp.dot(
        spread, parents_ref[...].astype(jnp.float32), preferred_element_type=jnp.float32
    ).astype(jnp.int32)
    equal = tiled == row // 8
    child_lane = lax.broadcasted_iota(jnp.int32, (128, 16), 1)
    chosen = child_lane == me * 4 + row // 8
    target = jnp.sum(jnp.where(chosen, tiled, 0), axis=1, keepdims=True) * 8 + row % 8

    def wanted(mask):
        hit = equal & (child_owner == (owner ^ mask))
        return jnp.max(jnp.where(hit, 1.0, 0.0), axis=1, keepdims=True)

    passed = wanted(3)
    crossing = wanted(2) * (1.0 - passed)
    beside = wanted(1)
    lane = lax.broadcasted_iota(jnp.int32, (128, 128), 1)
    down = lax.broadcasted_iota(jnp.int32, (128, 128), 0)
    flags = jnp.where(
        lane == 0, passed, jnp.where(lane == 1, crossing, jnp.where(lane == 2, beside, 0.0))
    )
    same = lane // 32 == down // 32
    before = jnp.where(same & (lane < down), 1.0, 0.0)
    ahead = jnp.dot(before, flags, preferred_element_type=jnp.float32)
    totals = jnp.dot(jnp.where(same, 1.0, 0.0), flags, preferred_element_type=jnp.float32)
    x_slot = jnp.where(
        passed > 0.0,
        ahead[:, 0:1],
        jnp.where(crossing > 0.0, totals[:, 0:1] + ahead[:, 1:2], -1.0),
    ).astype(jnp.int32)
    o_slot = jnp.where(beside > 0.0, ahead[:, 2:3], -1.0).astype(jnp.int32)
    mine = owner == me
    local = row % 32

    def listing(slot_of):
        hit = (slot_of == lane) & mine
        return jnp.max(jnp.where(hit, local, -1), axis=0, keepdims=True)

    place = jnp.where(
        mine,
        local,
        jnp.where(
            owner == (me ^ 2),
            32 + x_slot,
            jnp.where(owner == (me ^ 1), 64 + o_slot, 96 + x_slot),
        ),
    )
    place_across = jnp.sum(jnp.where(lane == down, place, 0), axis=0, keepdims=True)
    code_down = jnp.sum(jnp.where(lane == target, place_across, 0), axis=1, keepdims=True)
    code = jnp.sum(jnp.where(lane == down, code_down, 0), axis=0, keepdims=True)
    x_most = jnp.max(totals[:, 0:1] + totals[:, 1:2], axis=0, keepdims=True)
    f_most = jnp.max(totals[:, 0:1], axis=0, keepdims=True)
    o_most = jnp.max(totals[:, 2:3], axis=0, keepdims=True)
    tier = jnp.zeros((1, 1), jnp.int32)
    for c, f, o in TIERS[:-1]:
        over = (x_most > float(c)) | (f_most > float(f)) | (o_most > float(o))
        tier += jnp.where(over, 1, 0)
    handed = jnp.full((1, 1), TIERS[-1][1], jnp.int32)
    for index in range(len(TIERS) - 1):
        handed = jnp.where(tier == index, TIERS[index][1], handed)
    child = row < 32
    late = child & ((code_down >= 96) | ((code_down >= 32 + handed) & (code_down < 64)))
    early = child & jnp.logical_not(late)
    groups = jnp.where(
        lane == 0, jnp.where(early, 1.0, 0.0), jnp.where(lane == 1, jnp.where(late, 1.0, 0.0), 0.0)
    )
    earlier = jnp.where(lane < down, 1.0, 0.0)
    position = jnp.dot(earlier, groups, preferred_element_type=jnp.float32).astype(jnp.int32)
    amount = jnp.sum(groups, axis=0, keepdims=True).astype(jnp.int32)

    def members(index, group):
        hit = (position[:, index : index + 1] == lane) & group
        return jnp.max(jnp.where(hit, row, -1), axis=0, keepdims=True)

    plan[0:1, :] = listing(x_slot)
    plan[1:2, :] = listing(o_slot)
    plan[2:3, :] = code
    plan[3:4, :] = jnp.broadcast_to(tier, (1, 128))
    plan[4:5, :] = members(0, early)
    plan[5:6, :] = members(1, late)
    plan[6:7, :] = amount
    plan[7:8, :] = jnp.ones((1, 128), jnp.int32)


def make_plan(parents, me):
    return pl.pallas_call(
        plan_kernel,
        in_specs=[pl.BlockSpec(memory_space=pltpu.SMEM), pl.BlockSpec(memory_space=pltpu.VMEM)],
        out_specs=pl.BlockSpec(memory_space=pltpu.VMEM),
        out_shape=jax.ShapeDtypeStruct((8, 128), jnp.int32),
        name="plan",
    )(me.reshape(1), parents)


def attend_kernel(heads, q_ref, k_ref, v_ref, lo_ref, hi_ref, *outs):
    lo = jnp.concatenate([lo_ref[0]] * GROUP, axis=0)
    hi = jnp.concatenate([hi_ref[0]] * GROUP, axis=0)
    beams, _, length, _ = k_ref.shape
    keys = beams * length
    column = lax.broadcasted_iota(jnp.int32, (16 * GROUP, keys), 1)
    live = (column >= lo) & (column < hi)
    local = (hi > lo).astype(jnp.float32)
    scale = HEAD_DIM**-0.5
    width = GROUP * HEAD_DIM
    key_base = heads * width
    value_base = key_base + heads * HEAD_DIM
    for k in range(heads):
        q = jnp.concatenate(
            [
                q_ref[0, :, k * width + g * HEAD_DIM : k * width + (g + 1) * HEAD_DIM]
                for g in range(GROUP)
            ],
            axis=0,
        )
        head = slice(k * HEAD_DIM, (k + 1) * HEAD_DIM)
        keys_here = k_ref[:, 0, :, head].reshape(keys, HEAD_DIM)
        values_here = v_ref[:, 0, :, head].reshape(keys, HEAD_DIM)
        new_key = q_ref[0, :, key_base + k * HEAD_DIM : key_base + (k + 1) * HEAD_DIM]
        new_value = q_ref[0, :, value_base + k * HEAD_DIM : value_base + (k + 1) * HEAD_DIM]
        scores = (
            lax.dot_general(
                q, keys_here, (((1,), (1,)), ((), ())), preferred_element_type=jnp.float32
            )
            * scale
        )
        new_keys = jnp.concatenate([new_key.astype(jnp.float32)] * GROUP, axis=0)
        new_values = jnp.concatenate([new_value.astype(jnp.float32)] * GROUP, axis=0)
        fresh = jnp.sum(q.astype(jnp.float32) * new_keys, axis=1, keepdims=True) * scale
        scores = jnp.where(live, scores, big_negative)
        top = jnp.maximum(jnp.max(scores, axis=1, keepdims=True), fresh)
        weights = jnp.exp(scores - top)
        fresh_weight = jnp.exp(fresh - top)
        share = 1.0 / (jnp.sum(weights, axis=1, keepdims=True) + fresh_weight)
        half = (weights * share).astype(jnp.bfloat16)
        fresh_half = (fresh_weight * share).astype(jnp.bfloat16).astype(jnp.float32)
        mixed = jnp.dot(half, values_here, preferred_element_type=jnp.float32)
        mixed = jnp.where(local > 0.0, mixed + fresh_half * new_values, 0.0).astype(jnp.bfloat16)
        for block in range(4):
            out = outs[block % 2]
            for g in range(GROUP):
                out[block // 2, 0, :, k * width + g * HEAD_DIM : k * width + (g + 1) * HEAD_DIM] = mixed[
                    g * 16 + 4 * block : g * 16 + 4 * block + 4
                ]


def attend(queries, keys, values, lo, hi):
    prompts, children, width = queries.shape
    beams, _, length, depth = keys.shape
    heads = depth // HEAD_DIM
    wide = heads * GROUP * HEAD_DIM
    spec = pl.BlockSpec((beams, 1, length, depth), lambda p: (0, p, 0, 0))
    bound = pl.BlockSpec((1, children, 1), lambda p: (p, 0, 0))
    return pl.pallas_call(
        functools.partial(attend_kernel, heads),
        grid=(prompts,),
        in_specs=[pl.BlockSpec((1, children, width), lambda p: (p, 0, 0)), spec, spec, bound, bound],
        out_specs=[pl.BlockSpec((2, 1, 4, wide), lambda p: (0, p, 0, 0))] * 2,
        out_shape=[jax.ShapeDtypeStruct((2, prompts, 4, wide), jnp.bfloat16)] * 2,
        compiler_params=pltpu.CompilerParams(vmem_limit_bytes=VMEM),
        cost_estimate=TINY,
        name="attend",
    )(queries, keys, values, lo, hi)


def one_hot(column, width):
    lane = lax.broadcasted_iota(jnp.int32, (column.shape[0], width), 1)
    return (lane == column).astype(jnp.bfloat16)


def pick(column, table):
    return jnp.dot(one_hot(column, table.shape[0]), table, preferred_element_type=jnp.float32)


def pack_taps_kernel(*refs):
    half = len(refs) // 2
    taps = refs[half][...]
    for column, out in zip(refs[:half], refs[half + 1 :]):
        out[...] = pick(column[...], taps).astype(jnp.bfloat16)


def pack_taps(tier, plan, taps):
    c, f, o = tier
    width = taps.shape[1]
    listings = [plan[0, :c], plan[1, :o]] + ([plan[0, :f]] if c > f else [])
    columns = [
        jnp.concatenate(
            [jnp.where(base >= 0, base // 8 * 24 + 8 * k + base % 8, -1) for k in range(3)]
        )[:, None]
        for base in listings
    ]
    vmem = pl.BlockSpec(memory_space=pltpu.VMEM)
    outs = pl.pallas_call(
        pack_taps_kernel,
        in_specs=[vmem] * (len(columns) + 1),
        out_specs=[vmem] * len(columns),
        out_shape=[jax.ShapeDtypeStruct((x.shape[0], width), jnp.bfloat16) for x in columns],
        compiler_params=pltpu.CompilerParams(vmem_limit_bytes=VMEM),
        cost_estimate=TINY,
        name="pack_taps",
    )(*columns, taps)
    return outs if c > f else (*outs, outs[0])


def pack_kernel(tier, plan, state, *rest):
    c, f, o = tier
    sems = rest[-1]
    xa, out = rest[0], rest[-2]

    def copies(which, first, count, target, base):
        def start(s, _):
            row = jnp.maximum(plan[which, first + s], 0)
            pltpu.make_async_copy(state.at[row], target.at[s], sems.at[base + s]).start()
            return 0

        lax.fori_loop(0, count, start, 0)

    copies(0, 0, f, xa, 0)
    copies(1, 0, o, out, c)
    if c > f:
        copies(0, f, c - f, rest[1], f)

    def finish(s, _):
        pltpu.make_async_copy(state.at[0], xa.at[0], sems.at[s]).wait()
        return 0

    lax.fori_loop(0, c + o, finish, 0)


def pack(tier, plan, state):
    c, f, o = tier
    rows = [f] + ([c - f] if c > f else []) + [o]
    vmem = pl.BlockSpec(memory_space=pltpu.VMEM)
    anywhere = pl.BlockSpec(memory_space=pl.ANY)
    outs = pl.pallas_call(
        functools.partial(pack_kernel, tier),
        in_specs=[pl.BlockSpec(memory_space=pltpu.SMEM), vmem],
        out_specs=[anywhere] * len(rows),
        out_shape=[jax.ShapeDtypeStruct((n,) + state.shape[1:], jnp.bfloat16) for n in rows],
        scratch_shapes=[pltpu.SemaphoreType.DMA((c + o,))],
        compiler_params=pltpu.CompilerParams(vmem_limit_bytes=VMEM),
        cost_estimate=TINY,
        name="pack",
    )(plan, state)
    if c == f:
        return outs[0], None, outs[1]
    return outs


def conv_kernel(code, token, weight, bias, select, taps, *rest):
    *tables, conv_out, next_taps, partial = rest
    count = token.shape[0]
    code = code[...]
    tap = lax.broadcasted_iota(jnp.int32, (3 * count, 1), 0) // count

    def part(base, table):
        size = table.shape[0] // 3
        slot = code - base
        inside = (slot >= 0) & (slot < size)
        return pick(jnp.where(inside, slot + tap * size, -1), table[...])

    window = pick(jnp.where(code < 32, code // 8 * 24 + tap * 8 + code % 8, -1), taps[...])
    for index, table in enumerate(tables):
        window += part(32 * (index + 1), table)
    fresh = token[...]
    for start in range(0, count, 8):
        for k, source in enumerate((window[count : 2 * count], window[2 * count :], fresh)):
            next_taps[3 * start + 8 * k : 3 * start + 8 * k + 8, :] = source[
                start : start + 8
            ].astype(jnp.bfloat16)
    w = weight[...].astype(jnp.float32)
    total = window[:count] * w[0:1]
    total += window[count : 2 * count] * w[1:2]
    total += window[2 * count :] * w[2:3]
    total += fresh.astype(jnp.float32) * w[3:4]
    v = total + bias[...]
    conv = v / (1.0 + jnp.exp(-v))
    conv_out[...] = conv
    partial[...] = lax.dot_general(
        conv.astype(jnp.bfloat16),
        select[...],
        (((1,), (1,)), ((), ())),
        preferred_element_type=jnp.float32,
    )


def convolve(code, token, weight, bias, select, taps, tables):
    count, width = token.shape
    vmem = pl.BlockSpec(memory_space=pltpu.VMEM)
    return pl.pallas_call(
        conv_kernel,
        in_specs=[vmem] * (6 + len(tables)),
        out_specs=[vmem] * 3,
        out_shape=[
            jax.ShapeDtypeStruct((count, width), jnp.float32),
            jax.ShapeDtypeStruct((3 * count, width), jnp.bfloat16),
            jax.ShapeDtypeStruct((count, select.shape[0]), jnp.float32),
        ],
        compiler_params=pltpu.CompilerParams(vmem_limit_bytes=VMEM),
        cost_estimate=TINY,
        name="convolve",
    )(code, token, weight, bias, select, taps, *tables)


def step_kernel(projected, across, gain, weight, bias, step, b_wide, c_wide):
    rank = gain.shape[1]
    raw = projected[:, :rank]
    mean = jnp.mean(raw * raw, axis=1, keepdims=True)
    norm = (raw * lax.rsqrt(mean + 1e-06) * gain[...]).astype(jnp.bfloat16)
    v = jnp.dot(norm, weight[...], preferred_element_type=jnp.float32) + bias[...]
    step[...] = jnp.maximum(v, 0.0) + jnp.log1p(jnp.exp(-jnp.abs(v)))
    states = b_wide.shape[1]
    for r in range(b_wide.shape[0]):
        b_wide[r] = jnp.broadcast_to(across[:states, r : r + 1], b_wide.shape[1:])
        c_wide[r] = jnp.broadcast_to(across[states:, r : r + 1], c_wide.shape[1:])


def step_sizes(projected, gain, weight, bias):
    count, width = projected.shape[0], weight.shape[1]
    rank = gain.shape[1]
    across = projected[:, rank:].T
    states = across.shape[0] // 2
    vmem = pl.BlockSpec(memory_space=pltpu.VMEM)
    wide = jax.ShapeDtypeStruct((count, states, 128), jnp.float32)
    return pl.pallas_call(
        step_kernel,
        in_specs=[vmem] * 5,
        out_specs=[vmem] * 3,
        out_shape=[jax.ShapeDtypeStruct((count, width), jnp.float32), wide, wide],
        compiler_params=pltpu.CompilerParams(vmem_limit_bytes=VMEM),
        cost_estimate=TINY,
        name="step_sizes",
    )(projected, across, gain, weight, bias)


def advance(plan, which, starts, step, conv, rates, b_in, c_in, held, done, lines, next_state, sems):
    total = plan[6, which]
    in_sems, out_sems = sems

    def begin(n, _):
        r = plan[4 + which, n]
        where = plan[2, r]
        for condition, source, base in starts:

            @pl.when(condition(where))
            def _(source=source, base=base):
                pltpu.make_async_copy(source.at[where - base], held.at[n], in_sems.at[n]).start()

        return 0

    lax.fori_loop(0, total, begin, 0)
    def one(n):
        valid = n < total
        r = jnp.maximum(plan[4 + which, n], 0)

        @pl.when(valid)
        def _():
            pltpu.make_async_copy(next_state.at[0], held.at[n], in_sems.at[n]).wait()

        b = b_in[r]
        c_out = c_in[r]
        sizes = step[pl.ds(r, 1), :]
        gains = sizes * conv[pl.ds(r, 1), :]
        readouts = []
        for first in range(0, step.shape[1], 128):
            part = slice(first, first + 128)
            state = held[n, :, part].astype(jnp.float32)
            new = jnp.exp(-sizes[:, part] * rates[:, part]) * state + gains[:, part] * b
            done[n, :, part] = new.astype(jnp.bfloat16)
            readouts.append(jnp.sum(c_out * new, axis=0, keepdims=True))
        return valid, r, jnp.concatenate(readouts, axis=1)

    def work(m, _):
        rows = [one(2 * m), one(2 * m + 1)]
        for offset, (valid, r, readout) in enumerate(rows):
            n = 2 * m + offset

            @pl.when(valid)
            def _(r=r, n=n, readout=readout):
                lines[pl.ds(r, 1), :] = lines[pl.ds(r, 1), :] + readout
                pltpu.make_async_copy(done.at[n], next_state.at[r], out_sems.at[n]).start()

        return 0

    lax.fori_loop(0, (total + 1) // 2, work, 0)

    def finish(n, _):
        pltpu.make_async_copy(done.at[n], next_state.at[0], out_sems.at[n]).wait()
        return 0

    lax.fori_loop(0, total, finish, 0)


def early_kernel(
    tier, plan, step, conv, decay_log, skip, gate, b_in, c_in, local, xa, beside, next_state, lines, opened, held, done, rates, *sems
):
    f = tier[1]
    rates[...] = jnp.exp(decay_log[...])
    lines[...] = skip[...] * conv[...]
    gates = gate[...].astype(jnp.float32)
    opened[...] = gates / (1.0 + jnp.exp(-gates))
    starts = (
        (lambda w: w < 32, local, 0),
        (lambda w: (w >= 32) & (w < 32 + f), xa, 32),
        (lambda w: (w >= 64) & (w < 96), beside, 64),
    )
    advance(plan, 0, starts, step, conv, rates, b_in, c_in, held, done, lines, next_state, sems)


def late_kernel(
    tier, has_xb, plan, step, conv, decay_log, b_in, c_in, lines_in, opened, *rest
):
    f = tier[1]
    sources, rest = rest[: 2 if has_xb else 1], rest[2 if has_xb else 1 :]
    _, next_state, output, held, done, rates, lines, *sems = rest
    rates[...] = jnp.exp(decay_log[...])
    lines[...] = lines_in[...]
    starts = [(lambda w: w >= 96, sources[-1], 96)]
    if has_xb:
        starts.append((lambda w: w < 96, sources[0], 32 + f))
    advance(plan, 1, starts, step, conv, rates, b_in, c_in, held, done, lines, next_state, sems)
    output[...] = (lines[...] * opened[...]).astype(jnp.bfloat16)


def scan_scratch(count, states, width):
    return [
        pltpu.VMEM((count, states, width), jnp.bfloat16),
        pltpu.VMEM((count, states, width), jnp.bfloat16),
        pltpu.VMEM((states, width), jnp.float32),
    ], [pltpu.SemaphoreType.DMA((count,)), pltpu.SemaphoreType.DMA((count,))]


def early(tier, plan, step, conv, decay_log, skip, gate, b_in, c_in, local, xa, beside):
    count, width = step.shape
    states = decay_log.shape[0]
    vmem = pl.BlockSpec(memory_space=pltpu.VMEM)
    anywhere = pl.BlockSpec(memory_space=pl.ANY)
    arrays, sems = scan_scratch(count, states, width)
    return pl.pallas_call(
        functools.partial(early_kernel, tier),
        in_specs=[pl.BlockSpec(memory_space=pltpu.SMEM)] + [vmem] * 7 + [anywhere] * 3,
        out_specs=[anywhere, vmem, vmem],
        out_shape=[
            jax.ShapeDtypeStruct((count, states, width), jnp.bfloat16),
            jax.ShapeDtypeStruct((count, width), jnp.float32),
            jax.ShapeDtypeStruct((count, width), jnp.float32),
        ],
        scratch_shapes=arrays + sems,
        compiler_params=pltpu.CompilerParams(vmem_limit_bytes=VMEM),
        cost_estimate=TINY,
        name="early",
    )(plan, step, conv, decay_log, skip, gate, b_in, c_in, local, xa, beside)


def late(tier, plan, step, conv, decay_log, b_in, c_in, lines, opened, buffers, next_state):
    count, width = step.shape
    states = decay_log.shape[0]
    vmem = pl.BlockSpec(memory_space=pltpu.VMEM)
    anywhere = pl.BlockSpec(memory_space=pl.ANY)
    arrays, sems = scan_scratch(count, states, width)
    return pl.pallas_call(
        functools.partial(late_kernel, tier, len(buffers) == 2),
        in_specs=[pl.BlockSpec(memory_space=pltpu.SMEM)]
        + [vmem] * 7
        + [anywhere] * (len(buffers) + 1),
        out_specs=[anywhere, vmem],
        out_shape=[
            jax.ShapeDtypeStruct((count, states, width), jnp.bfloat16),
            jax.ShapeDtypeStruct((count, width), jnp.bfloat16),
        ],
        scratch_shapes=arrays + [pltpu.VMEM((count, width), jnp.float32)] + sems,
        input_output_aliases={8 + len(buffers): 0},
        compiler_params=pltpu.CompilerParams(vmem_limit_bytes=VMEM),
        cost_estimate=TINY,
        name="late",
    )(plan, step, conv, decay_log, b_in, c_in, lines, opened, *buffers, next_state)


def across_chips(x):
    others = [lax.ppermute(x, ("tensor", "sub"), pairs(mask)) for mask in (1, 2, 3)]
    return x, *others


def quick_body(
    token_input,
    gate_input,
    conv_taps,
    scan_state,
    conv_weight,
    conv_bias,
    select_weight,
    step_gain,
    step_weight,
    step_bias,
    decay_log,
    skip_gain,
    query,
    fresh_key,
    fresh_value,
    key_cache,
    value_cache,
    cache_lengths,
    parents,
):
    me = lax.axis_index("dp")
    beams, prompts, width = token_input.shape
    states, rank = decay_log.shape[0], step_gain.shape[0]
    count = beams * prompts
    cache_prompts, length = key_cache.shape[1], key_cache.shape[2]
    first = lax.axis_index("sub") * cache_prompts

    plan = make_plan(parents, me)
    asked = jnp.concatenate([query, fresh_key, fresh_value], axis=2)
    asked = [asked, send(asked, 1), send(asked, 2)]
    taps = conv_taps.transpose(0, 2, 1, 3).reshape(3 * count, width)
    state = scan_state.reshape(count, states, width)

    def bounds():
        here = lax.dynamic_slice_in_dim(parents, first, cache_prompts, 0)
        lengths = lax.dynamic_slice_in_dim(cache_lengths, first, cache_prompts, 1)
        related = jnp.concatenate(
            [lax.dynamic_slice_in_dim(here, (me ^ mask) * beams, beams, 1) for mask in range(4)], axis=1
        )
        live = jnp.sum(
            jnp.where(
                related[:, :, None] == np.arange(16)[None, None, :], lengths.T[:, None, :], 0
            ),
            axis=2,
        )
        local = related // beams == me
        lo = jnp.where(local, (related % beams) * length, 0)
        hi = jnp.where(local, lo + live, 0)
        return lo[:, :, None], hi[:, :, None]

    def middle(plan, taps, tables, asked):
        conv, next_taps, partial = convolve(
            jnp.tile(plan[2, :count], 3)[:, None],
            token_input.reshape(count, width),
            conv_weight,
            conv_bias[None],
            select_weight.T,
            taps,
            tables,
        )
        shares = across_chips(partial)
        queries = jnp.concatenate(asked, axis=0).transpose(1, 0, 2)
        outs = attend(queries, key_cache, value_cache, *bounds())
        shares, outs = lax.optimization_barrier((shares, outs))
        beside = send(outs[1], 1)
        projected = (shares[0] + shares[1]) + (shares[2] + shares[3])
        step, b_in, c_in = step_sizes(projected, step_gain[None], step_weight, step_bias[None])
        back = outs[0][1] + beside[1]
        return lax.optimization_barrier(
            (conv, next_taps, step, b_in, c_in, back, outs[0][0], beside[0])
        )

    def skipped(plan, taps, tables, asked):
        shapes = jax.eval_shape(middle, plan, taps, tables, asked)
        return jax.tree.map(lambda x: jnp.zeros(x.shape, x.dtype), shapes)

    def run(limits):
        c, f, o = limits

        def branch(plan, taps, state, asked):
            asked = [*asked, send(asked[2], 1)]
            tx, to, tf = pack_taps(limits, plan, taps)
            tables = [send(tx, 2), send(to, 1), send(tf, 3)]
            xa, xb, near = pack(limits, plan, state)
            near = send(near, 1)
            xa, tables, asked = lax.optimization_barrier((xa, tables, asked))
            xa = send(xa, 2)
            conv, next_taps, step, b_in, c_in, back, own, beside = lax.cond(
                plan[7, 0] == 1, middle, skipped, plan, taps, tables, asked
            )
            second = [back] if xb is None else [back, xb]
            xa, near, step, *second = lax.optimization_barrier((xa, near, step, *second))
            passed = send(xa, 1)
            buffers = [passed] if xb is None else [send(second[1], 2), passed]
            attention = (own + beside + send(second[0], 2)).transpose(1, 0, 2)
            next_state, lines, opened = early(
                limits,
                plan,
                step,
                conv,
                decay_log,
                skip_gain[None],
                gate_input.reshape(count, width),
                b_in,
                c_in,
                state,
                xa,
                near,
            )
            next_state, output = late(
                limits, plan, step, conv, decay_log, b_in, c_in, lines, opened, buffers, next_state
            )
            return next_state, next_taps, output, attention

        return branch

    next_state, next_taps, output, attention = lax.switch(
        plan[3, 0],
        [run(limits) for limits in TIERS],
        plan,
        taps,
        state,
        asked,
    )
    return (
        next_state.reshape(beams, prompts, states, width),
        next_taps.reshape(beams, 3, prompts, width).transpose(0, 2, 1, 3),
        output.reshape(beams, prompts, width),
        attention,
    )


def choose_rows(array, picks):
    index = picks.reshape(picks.shape + (1,) * (array.ndim - 2))
    return jnp.take_along_axis(array, index, axis=0)


def parent_rows(parents, first, count):
    return lax.dynamic_slice_in_dim(parents, first, count, 0).T


def general_body(
    token_input,
    gate_input,
    conv_taps,
    scan_state,
    conv_weight,
    conv_bias,
    select_weight,
    step_gain,
    step_weight,
    step_bias,
    decay_log,
    skip_gain,
    query,
    fresh_key,
    fresh_value,
    key_cache,
    value_cache,
    cache_lengths,
    parents,
):
    group_width = lax.axis_size("dp")
    my_index = lax.axis_index("dp")
    sub_index = lax.axis_index("sub")
    beam_slots = token_input.shape[0]
    prompt_count = token_input.shape[1]
    prompt_share = prompt_count // group_width
    cache_prompts = key_cache.shape[1]
    cache_share = cache_prompts // group_width
    cache_base = sub_index * cache_prompts
    cache_length = key_cache.shape[2]
    group_size = HEADS // KV_HEADS
    score_scale = HEAD_DIM ** (-0.5)
    heads_local = query.shape[2] // HEAD_DIM
    kv_local = fresh_key.shape[2] // HEAD_DIM
    state_picks = parent_rows(parents, my_index * prompt_share, prompt_share)
    cache_picks = parent_rows(parents, cache_base + my_index * cache_share, cache_share)
    local_lengths = lax.dynamic_slice_in_dim(cache_lengths, cache_base, cache_prompts, 1)
    prompt_parents = parent_rows(parents, cache_base, cache_prompts)
    positions = jnp.arange(cache_length, dtype=jnp.int32)
    arrived = (
        lax.all_to_all(conv_taps, "dp", split_axis=1, concat_axis=0, tiled=True),
        lax.all_to_all(scan_state, "dp", split_axis=1, concat_axis=0, tiled=True),
        lax.all_to_all(key_cache, "dp", split_axis=1, concat_axis=0, tiled=True),
        lax.all_to_all(value_cache, "dp", split_axis=1, concat_axis=0, tiled=True),
    )
    parent_taps, parent_state, parent_keys, parent_values = (
        lax.all_to_all(
            choose_rows(arrived[0], state_picks), "dp", split_axis=0, concat_axis=1, tiled=True
        ),
        lax.all_to_all(
            choose_rows(arrived[1], state_picks), "dp", split_axis=0, concat_axis=1, tiled=True
        ),
        lax.all_to_all(
            choose_rows(arrived[2], cache_picks), "dp", split_axis=0, concat_axis=1, tiled=True
        ),
        lax.all_to_all(
            choose_rows(arrived[3], cache_picks), "dp", split_axis=0, concat_axis=1, tiled=True
        ),
    )
    children = lax.dynamic_slice_in_dim(prompt_parents, my_index * beam_slots, beam_slots, 0)
    parent_length = jnp.take_along_axis(local_lengths, children, axis=0)
    queries = query.reshape((beam_slots, cache_prompts, kv_local, group_size, HEAD_DIM))
    new_keys = fresh_key.reshape((beam_slots, cache_prompts, kv_local, HEAD_DIM))
    new_values = fresh_value.reshape((beam_slots, cache_prompts, kv_local, HEAD_DIM))
    keys_split = parent_keys.reshape((beam_slots, cache_prompts, cache_length, kv_local, HEAD_DIM))
    values_split = parent_values.reshape(
        (beam_slots, cache_prompts, cache_length, kv_local, HEAD_DIM)
    )
    scores = (
        jnp.einsum("rpkgd,rptkd->rpkgt", queries, keys_split, preferred_element_type=jnp.float32)
        * score_scale
    )
    live_mask = positions[None, None, None, None, :] < parent_length[:, :, None, None, None]
    fresh_score = (
        jnp.einsum("rpkgd,rpkd->rpkg", queries, new_keys, preferred_element_type=jnp.float32)
        * score_scale
    )
    row_max = jnp.maximum(jnp.max(jnp.where(live_mask, scores, big_negative), axis=-1), fresh_score)
    weights = jnp.where(live_mask, jnp.exp(scores - row_max[..., None]), 0.0)
    fresh_weight = jnp.exp(fresh_score - row_max)
    row_total = jnp.sum(weights, axis=-1) + fresh_weight
    weights_half = (weights / row_total[..., None]).astype(jnp.bfloat16)
    fresh_half = (fresh_weight / row_total).astype(jnp.bfloat16)
    attended = jnp.einsum(
        "rpkgt,rptkd->rpkgd", weights_half, values_split, preferred_element_type=jnp.float32
    )
    attended = (
        attended
        + fresh_half.astype(jnp.float32)[..., None]
        * new_values.astype(jnp.float32)[:, :, :, None, :]
    )
    attention_output = attended.reshape((beam_slots, cache_prompts, heads_local * HEAD_DIM)).astype(
        jnp.bfloat16
    )
    window = jnp.concatenate([parent_taps, token_input[:, :, None, :]], axis=2)
    conv_output = jax.nn.silu(
        jnp.sum(window.astype(jnp.float32) * conv_weight.astype(jnp.float32), axis=2) + conv_bias
    )
    conv_half = conv_output.astype(jnp.bfloat16)
    partial_sums = jnp.einsum(
        "bpc,cr->bpr", conv_half, select_weight, preferred_element_type=jnp.float32
    )
    projected = lax.psum(partial_sums, ("tensor", "sub"))
    rank_size = step_gain.shape[0]
    state_size = decay_log.shape[0]
    step_raw = projected[..., :rank_size]
    state_input = projected[..., rank_size : rank_size + state_size]
    state_readout = projected[..., rank_size + state_size :]
    step_norm = (
        step_raw
        * lax.rsqrt(jnp.mean(step_raw * step_raw, axis=-1, keepdims=True) + 1e-06)
        * step_gain
    ).astype(jnp.bfloat16)
    step_size = jax.nn.softplus(
        jnp.einsum("bpr,rc->bpc", step_norm, step_weight, preferred_element_type=jnp.float32)
        + step_bias
    )
    decay_factor = jnp.exp(-step_size[:, :, None, :] * jnp.exp(decay_log)[None, None])
    state_next = (
        decay_factor * parent_state.astype(jnp.float32)
        + step_size[:, :, None, :] * state_input[..., None] * conv_output[:, :, None, :]
    )
    readout = jnp.sum(state_readout[..., None] * state_next, axis=2) + skip_gain * conv_output
    mamba_output = (readout * jax.nn.silu(gate_input.astype(jnp.float32))).astype(jnp.bfloat16)
    return (state_next.astype(jnp.bfloat16), window[:, :, 1:, :], mamba_output, attention_output)


def body(*arrays):
    token_input, parents = arrays[0], arrays[-1]
    sizes = (lax.axis_size("dp"), token_input.shape[0], token_input.shape[1], parents.shape[1])
    paired = lax.axis_size("tensor") == 2 and lax.axis_size("sub") == 2
    if sizes == (4, 4, 8, 16) and paired:
        return quick_body(*arrays)
    return general_body(*arrays)


def solution(mesh):
    placed = (
        P("dp", "groups", ("tensor", "sub")),
        P("dp", "groups", ("tensor", "sub")),
        P("dp", "groups", None, ("tensor", "sub")),
        P("dp", "groups", None, ("tensor", "sub")),
        P(None, ("tensor", "sub")),
        P(("tensor", "sub")),
        P(("tensor", "sub"), None),
        P(),
        P(None, ("tensor", "sub")),
        P(("tensor", "sub")),
        P(None, ("tensor", "sub")),
        P(("tensor", "sub")),
        P("dp", ("groups", "sub"), "tensor"),
        P("dp", ("groups", "sub"), "tensor"),
        P("dp", ("groups", "sub"), "tensor"),
        P("dp", ("groups", "sub"), None, "tensor"),
        P("dp", ("groups", "sub"), None, "tensor"),
        P(None, "groups"),
        P("groups", None),
    )
    return jax.shard_map(
        body,
        mesh=mesh,
        in_specs=placed,
        out_specs=(
            P("dp", "groups", None, ("tensor", "sub")),
            P("dp", "groups", None, ("tensor", "sub")),
            P("dp", "groups", ("tensor", "sub")),
            P("dp", ("groups", "sub"), "tensor"),
        ),
        check_vma=False,
    )
```
